32 devices in a mesh: groups: 2 (over y), slab: 16 (over z, x, core).
Axes of the slice: x: 2, y: 2, z: 4, core: 2. Of those that a mesh axis runs over, the one named last changes fastest.
Arguments:
- charges: bfloat16 [131072, 512], P(('groups', 'slab')), parts along dimension 0, may hold values from -6 to 6
- near_blocks: bfloat16 [1024, 3, 128, 128], P(('groups', 'slab')), parts along dimension 0, may hold values from -0.3125 to 0.3125
- near_pattern: int32 [1024, 3], P(('groups', 'slab')), parts along dimension 0, may hold values from 0 to 1, as said below
- leaf_basis: bfloat16 [1024, 64, 128], P(('groups', 'slab')), parts along dimension 0, may hold values from -0.5 to 0.5
- transfers: bfloat16 [992, 64, 128], P(('groups', 'slab')), parts along dimension 0, may hold values from -0.5 to 0.5
- couplings: bfloat16 [2016, 64, 256], P(('groups', 'slab')), parts along dimension 0, may hold values from -0.375 to 0.375
- interactions: int32 [2016, 4], P(('groups', 'slab')), parts along dimension 0, may hold values 0 or 1
Outputs:
- potentials: bfloat16 [131072, 512], P(('groups', 'slab')), parts along dimension 0
The draws below stay inside these ranges and needn't reach their ends.
There are 2 independent parts, one for each index of `groups`. The reference program is written for one: setup_inputs(seed, part) draws one part's arguments, and reference() takes and returns one part's arrays. A program takes and returns all parts, laid end to end along the dimension named above; each array names one. Nothing has to cross between parts.
Inputs may be any that keep to these rules, and one draw needn't show every extreme that they name: `near_pattern`: the middle column, a leaf's block with itself, is 1 for every leaf.
All inputs are finite; a program needn't handle non-finite values. No bound on the sum of `interactions` on one device may be relied on, other than what follows from the above.
Results may differ from the reference program's by a relative error of at most 0.0073.
Values may be sent and summed in bfloat16 or wider, within the bound.
No kernel may reach another device: no remote copies, remote signals or barrier semaphores. Data moves between devices by JAX's collectives and lax.ppermute only.
A program may use at most 128 MiB of HBM per device.

```python
import jax
import jax.numpy as jnp
from jax import lax

PANELS = 128
RANK = 64
NRHS = 512
LEVELS = 6
LEAF_DEV = 32
LEAVES = 512
COUPLE_BOXES = 1008
TRANS_BOXES = 496
N_SLAB = 16


def draw_near_pattern(key, part):
    key = jax.random.fold_in(key, 11)
    random_side = jax.random.randint(key, (LEAVES, 3), 0, 4)
    picked = jnp.where(random_side > 0, 1, 0).astype(jnp.int32)
    middle = jnp.arange(3)[None, :] == 1
    return jnp.where(middle, 1, picked).astype(jnp.int32)


def plant(result, own_key, smallest, high):
    longest = result.shape.index(max(result.shape))
    spots = []
    for shift in (0, 1):
        where = [jax.random.randint(jax.random.fold_in(own_key, axis), (), 0, length) for axis, length in enumerate(result.shape)]
        where[longest] = (where[longest] + shift) % result.shape[longest]
        spots.append(tuple(where))
    return result.at[spots[0]].set(smallest).at[spots[1]].set(high)


def level_of(rng, shape, cuts, smallest, largest):
    gain = 1.0
    for dim, parts in cuts:
        heights = jax.random.uniform(jax.random.fold_in(jax.random.fold_in(rng, 6), dim), (parts,), jnp.float32, smallest / len(cuts), largest / len(cuts))
        gain = gain * jnp.repeat(jnp.exp(heights), shape[dim] // parts).reshape((-1,) + (1,) * (len(shape) - 1 - dim))
    return gain


def gaussian(rng, shape, spread, bound, cuts=(), kind=jnp.bfloat16):
    factor_of = level_of(rng, shape, cuts, -0.22, 0.18) if cuts else 1.0
    values = jax.random.normal(rng, shape, jnp.float32) * spread * factor_of
    return jnp.minimum(jnp.maximum(values, -bound), bound).astype(kind)


def setup_inputs(seed: int = 0, part: int = 0) -> dict:
    splits = jax.random.split(jax.random.key(seed), 8)
    part_splits = jax.random.split(jax.random.fold_in(splits[7], part), 8)
    return {
        "charges": gaussian(part_splits[0], (LEAVES * PANELS, NRHS), 1.0, 6.0, ((0, 16),)),
        "near_blocks": gaussian(part_splits[1], (LEAVES, 3, PANELS, PANELS), (3 * PANELS) ** -0.5, 0.3125, ((0, 16),)),
        "near_pattern": draw_near_pattern(jax.random.fold_in(jax.random.fold_in(splits[7], part), 71), part),
        "leaf_basis": gaussian(part_splits[3], (LEAVES, RANK, PANELS), PANELS ** -0.5, 0.5, ((0, 16),)),
        "transfers": gaussian(part_splits[4], (TRANS_BOXES, RANK, 2 * RANK), (2 * RANK) ** -0.5, 0.5, ((0, 16),)),
        "couplings": gaussian(part_splits[5], (COUPLE_BOXES, RANK, 4 * RANK), (4 * RANK) ** -0.5, 0.375, ((0, 16),)),
        "interactions": plant((jax.random.randint(part_splits[6], (COUPLE_BOXES, 4), 0, 4) < 3).astype(jnp.int32), jax.random.fold_in(part_splits[6], 1), 0, 1),
    }


PRECISE = lax.Precision.HIGHEST
OFFSETS = (-3, -2, 2, 3)


def displaced(values, offset):
    total = values.shape[0]
    filler = jnp.zeros((abs(offset),) + values.shape[1:], values.dtype)
    if offset > 0:
        return jnp.concatenate([values[offset:], filler], axis=0)
    return jnp.concatenate([filler, values[:total + offset]], axis=0)


def level_slice(packed, first_box, box_count, trailing):
    grouped = packed.reshape((N_SLAB, -1) + trailing)
    return grouped[:, first_box:first_box + box_count].reshape((N_SLAB * box_count,) + trailing)


def rounded(values):
    narrow = lax.optimization_barrier(values.astype(jnp.bfloat16))
    return narrow.astype(jnp.float32)


def reference(charges, near_blocks, near_pattern, leaf_basis, transfers, couplings, interactions):
    source = charges.reshape(LEAVES, PANELS, NRHS).astype(jnp.float32)
    near_f = near_blocks.astype(jnp.float32)
    pattern = near_pattern.astype(jnp.float32)
    near_sum = jnp.zeros((LEAVES, PANELS, NRHS), jnp.float32)
    for column in range(3):
        offset = column - 1
        neighbour = source if offset == 0 else displaced(source, offset)
        product = jnp.einsum("ipq,iqr->ipr", near_f[:, column], neighbour, precision=PRECISE)
        near_sum = near_sum + product * pattern[:, column][:, None, None]
    basis_f = leaf_basis.astype(jnp.float32)
    multipoles = [rounded(jnp.einsum("ikp,ipr->ikr", basis_f, source, precision=PRECISE))]
    transfer_f = transfers.astype(jnp.float32)
    transfer_levels = []
    first_box = 0
    for tree_level in range(1, LEVELS):
        box_count = LEAF_DEV >> tree_level
        matrix = level_slice(transfer_f, first_box, box_count, (RANK, 2 * RANK))
        first_box += box_count
        transfer_levels.append(matrix)
        children = multipoles[-1].reshape(-1, 2 * RANK, NRHS)
        multipoles.append(rounded(jnp.einsum("bkj,bjr->bkr", matrix, children, precision=PRECISE)))
    coupling_f = couplings.astype(jnp.float32)
    list_flags = interactions.astype(jnp.float32)
    expansions = []
    first_box = 0
    for tree_level in range(LEVELS):
        box_count = LEAF_DEV >> tree_level
        matrix = level_slice(coupling_f, first_box, box_count, (RANK, 4 * RANK))
        chosen = level_slice(list_flags, first_box, box_count, (4,))
        first_box += box_count
        pieces = []
        for column, offset in enumerate(OFFSETS):
            pieces.append(displaced(multipoles[tree_level], offset) * chosen[:, column][:, None, None])
        stacked = jnp.concatenate(pieces, axis=1)
        expansions.append(jnp.einsum("bkj,bjr->bkr", matrix, stacked, precision=PRECISE))
    for tree_level in range(LEVELS - 1, 0, -1):
        matrix = transfer_levels[tree_level - 1]
        pushed = jnp.einsum("bkj,bkr->bjr", matrix, rounded(expansions[tree_level]), precision=PRECISE)
        expansions[tree_level - 1] = expansions[tree_level - 1] + pushed.reshape(-1, RANK, NRHS)
    leaf_local = rounded(expansions[0])
    far_field = jnp.einsum("ikp,ikr->ipr", basis_f, leaf_local, precision=PRECISE)
    return (near_sum + far_field).astype(jnp.bfloat16).reshape(LEAVES * PANELS, NRHS)
```

```python
import jax
import jax.numpy as jnp
from jax import lax
from jax.experimental import pallas as pl
from jax.experimental.pallas import tpu as pltpu
from jax.sharding import PartitionSpec as P

LEVELS = 6
FULL = LEVELS - 2
BF = jnp.bfloat16
F32 = jnp.float32
MIB = 1 << 20


def resident(shape, dtype):
    return pltpu.VMEM(shape, dtype)


def keep(array):
    return pltpu.with_memory_space_constraint(array, pltpu.VMEM)


def stay(array):
    return pltpu.with_memory_space_constraint(array, pltpu.HBM)


def dot(a, b):
    return lax.dot_general(a, b, (((1,), (0,)), ((), ())), preferred_element_type=F32)


def dot_t(a, b):
    return lax.dot_general(a, b, (((0,), (0,)), ((), ())), preferred_element_type=F32)


class Plan:
    def __init__(self, leaves, panels, rank, rhs):
        self.leaves, self.panels, self.rank, self.rhs = leaves, panels, rank, rhs
        self.count = [leaves >> level for level in range(LEVELS)]
        self.first = [sum(self.count[:level]) for level in range(LEVELS)]
        self.trans = [0] + [sum(self.count[1:level]) for level in range(1, LEVELS)]
        self.padded = [sum(c + 6 for c in self.count[:level]) for level in range(FULL)]
        self.padded_boxes = sum(c + 6 for c in self.count[:FULL])
        self.inner_boxes = sum(self.count[:FULL])
        self.msg_pole = [panels + 2 * rank * level for level in range(FULL)]
        self.msg_top = panels + 2 * rank * FULL
        self.msg_trans = self.msg_top + rank
        self.msg_basis = self.msg_trans + rank
        self.basis_rows = rank * panels // rhs
        self.msg_rows = self.msg_basis + self.basis_rows


def upward_kernel(plan, chunks, charges, basis, transfers, padded_x, poles, up, down, up2, down2, top, bs, ts, sems):
    p, r = plan.panels, plan.rank
    per = plan.leaves // chunks
    copies = [
        pltpu.make_async_copy(basis, bs, sems.at[chunks]),
        pltpu.make_async_copy(transfers, ts, sems.at[chunks + 1]),
    ]
    for c in range(chunks):
        rows = per * p
        copies.append(
            pltpu.make_async_copy(
                charges.at[pl.ds(c * rows, rows)], padded_x.at[pl.ds(p + c * rows, rows)], sems.at[c]
            )
        )
    for copy in copies:
        copy.start()
    padded_x[pl.ds(0, p)] = jnp.zeros((p, plan.rhs), BF)
    padded_x[pl.ds(p * (plan.leaves + 1), p)] = jnp.zeros((p, plan.rhs), BF)
    for level in range(FULL):
        start = plan.padded[level] * r
        poles[pl.ds(start, 3 * r)] = jnp.zeros((3 * r, plan.rhs), BF)
        poles[pl.ds(start + (plan.count[level] + 3) * r, 3 * r)] = jnp.zeros((3 * r, plan.rhs), BF)
    copies[0].wait()
    copies[1].wait()

    held = {}

    def keep(level, box, value):
        held[level, box] = value
        n = plan.count[level]
        if level < FULL:
            poles[pl.ds((plan.padded[level] + 3 + box) * r, r)] = value
            if n - 3 <= box <= n - 2:
                up[pl.ds(plan.msg_pole[level] + (box - n + 3) * r, r)] = value
            if 1 <= box <= 2:
                down[pl.ds(plan.msg_pole[level] + (box - 1) * r, r)] = value
        elif level == FULL:
            if box == 0:
                up[pl.ds(plan.msg_top, r)] = value
                down2[pl.ds(0, r)] = value
            else:
                down[pl.ds(plan.msg_top, r)] = value
                up2[pl.ds(0, r)] = value
        else:
            up2[pl.ds(r, r)] = value
            down2[pl.ds(r, r)] = value
            top[...] = value

    def climb(level, box):
        pair = jnp.concatenate([held[level - 1, 2 * box], held[level - 1, 2 * box + 1]], axis=0)
        keep(level, box, dot(ts[plan.trans[level] + box], pair).astype(BF))

    for c in range(chunks):
        copies[2 + c].wait()
        for leaf in range(c * per, (c + 1) * per):
            x = padded_x[pl.ds(p * (leaf + 1), p)]
            keep(0, leaf, dot(bs[leaf], x).astype(BF))
            box = leaf
            for level in range(1, LEVELS):
                if box % 2 == 0:
                    break
                box //= 2
                climb(level, box)
    for message, leaf, last in ((up, plan.leaves - 1, True), (down, 0, False)):
        message[pl.ds(0, p)] = padded_x[pl.ds(p * (leaf + 1), p)]
        for level in range(1, FULL + 1):
            box = plan.count[level] - 1 if last else 0
            message[pl.ds(plan.msg_trans, r), pl.ds((level - 1) * p, p)] = ts[plan.trans[level] + box]
        for part in range(plan.rhs // p):
            rows = plan.basis_rows
            message[pl.ds(plan.msg_basis, rows), pl.ds(part * p, p)] = bs[leaf, pl.ds(part * rows, rows)]


def inner_kernel(
    plan, chunks, pattern, flags, padded_x, poles, near_blocks, couplings,
    near, local, masked, edge_near, nb, cb, sems,
):
    p, r = plan.panels, plan.rank
    per = plan.leaves // chunks
    coupling_copy = pltpu.make_async_copy(couplings, cb, sems.at[chunks])
    copies = [
        pltpu.make_async_copy(near_blocks.at[pl.ds(c * per, per)], nb.at[pl.ds(c * per, per)], sems.at[c])
        for c in range(chunks)
    ]
    coupling_copy.start()
    for copy in copies:
        copy.start()
    coupling_copy.wait()
    lane = lax.broadcasted_iota(jnp.int32, (r, 4 * r), 1)

    def mask(box):
        low = jnp.where(lane < r, flags[0, box], flags[1, box])
        high = jnp.where(lane < 3 * r, flags[2, box], flags[3, box])
        chosen = jnp.where(lane < 2 * r, low, high)
        value = cb[box] * chosen.astype(F32).astype(BF)
        masked[box] = value
        return value

    def couple(level):
        base = plan.padded[level]

        def one(box):
            row = (base + box) * r
            near_side = poles[pl.ds(pl.multiple_of(row, r), 2 * r)]
            far_side = poles[pl.ds(pl.multiple_of(row + 5 * r, r), 2 * r)]
            stack = jnp.concatenate([near_side, far_side], axis=0)
            index = plan.first[level] + box
            local[pl.ds(pl.multiple_of(index * r, r), r)] = dot(mask(index), stack)

        def pair(step, carry):
            for k in range(4):
                one(step * 4 + k)
            return carry

        lax.fori_loop(0, plan.count[level] // 4, pair, 0)

    for level in range(FULL):
        couple(level)
    for box in range(plan.inner_boxes, sum(plan.count)):
        mask(box)

    def side(leaf, slot):
        block = nb[leaf, slot]
        return jnp.where(pattern[slot, leaf] != 0, block, jnp.zeros_like(block))

    def near_one(leaf):
        row = pl.multiple_of(leaf * p, p)
        wide = jnp.concatenate([side(leaf, 0), nb[leaf, 1], side(leaf, 2)], axis=1)
        near[pl.ds(row, p)] = dot(wide, padded_x[pl.ds(row, 3 * p)])

    for c in range(chunks):
        copies[c].wait()

        def step(s, carry, c=c):
            for k in range(2):
                near_one(c * per + s * 2 + k)
            return carry

        lax.fori_loop(0, per // 2, step, 0)
    edge_near[0] = side(0, 0)
    edge_near[1] = side(plan.leaves - 1, 2)


def final_kernel(
    plan, near, local, masked, edge_near, bs, ts, below, above, below2, above2, below3, above3,
    out, loc, stage, sems,
):
    p, r, n = plan.panels, plan.rank, plan.leaves

    def edges(message, last):
        basis = jnp.concatenate(
            [message[pl.ds(plan.msg_basis, plan.basis_rows), pl.ds(k * p, p)] for k in range(plan.rhs // p)], axis=0
        )
        x = message[pl.ds(0, p)]
        rim = [dot(basis, x).astype(BF)]
        sent = [message[pl.ds(plan.msg_pole[level], 2 * r)] for level in range(FULL)]
        for level in range(1, FULL + 1):
            matrix = message[pl.ds(plan.msg_trans, r), pl.ds((level - 1) * p, p)]
            if last:
                pair = jnp.concatenate([sent[level - 1][r:], rim[-1]], axis=0)
            else:
                pair = jnp.concatenate([rim[-1], sent[level - 1][:r]], axis=0)
            rim.append(dot(matrix, pair).astype(BF))
        return x, rim, sent

    x_low, rim_low, sent_low = edges(below, True)
    x_high, rim_high, sent_high = edges(above, False)

    box = plan.first[LEVELS - 1]
    low = jnp.concatenate([below3[...], below2[pl.ds(r, r)]], axis=0)
    high = jnp.concatenate([above2[pl.ds(r, r)], above3[...]], axis=0)
    summit = dot(masked[box], jnp.concatenate([low, high], axis=0)).astype(BF)
    pushed = dot_t(ts[plan.trans[LEVELS - 1]], summit)
    top_low, top_high = below[pl.ds(plan.msg_top, r)], above[pl.ds(plan.msg_top, r)]
    second = []
    for k, stack in enumerate(
        (
            [below2[pl.ds(0, r)], top_low, rim_high[FULL], top_high],
            [top_low, rim_low[FULL], top_high, above2[pl.ds(0, r)]],
        )
    ):
        box = plan.first[FULL] + k
        gained = dot(masked[box], jnp.concatenate(stack, axis=0))
        second.append((gained + pushed[k * r : (k + 1) * r]).astype(BF))

    rims = []
    for level in range(FULL):
        first, m = plan.first[level], plan.count[level]
        low = jnp.concatenate([sent_low[level], rim_low[level]], axis=0)
        high = jnp.concatenate([rim_high[level], sent_high[level]], axis=0)
        gain = [
            (0, dot(masked[first, :, pl.ds(0, 2 * r)], low[: 2 * r])),
            (1, dot(masked[first + 1, :, pl.ds(0, 2 * r)], low[r:])),
            (2, dot(masked[first + 2, :, pl.ds(0, r)], low[2 * r :])),
            (m - 1, dot(masked[first + m - 1, :, pl.ds(2 * r, 2 * r)], high[r:])),
            (m - 2, dot(masked[first + m - 2, :, pl.ds(2 * r, 2 * r)], high[: 2 * r])),
            (m - 3, dot(masked[first + m - 3, :, pl.ds(3 * r, r)], high[:r])),
        ]
        sums = {}
        for place, value in gain:
            sums[place] = sums[place] + value if place in sums else value
        rims.append(sums)

    def gather(level, box, push):
        index = plan.first[level] + box
        value = local[pl.ds(index * r, r)] + push
        if box in rims[level]:
            value = value + rims[level][box]
        return value.astype(BF)

    current = second
    for level in range(FULL, 1, -1):
        lower = []
        for box, value in enumerate(current):
            push = dot_t(ts[plan.trans[level] + box], value)
            lower.append(gather(level - 1, 2 * box, push[:r]))
            lower.append(gather(level - 1, 2 * box + 1, push[r:]))
        current = lower

    writes = []
    for box, value in enumerate(current):
        push = dot_t(ts[plan.trans[1] + box], value)
        for k in range(2):
            leaf = 2 * box + k
            leaf_local = gather(0, leaf, push[k * r : (k + 1) * r])
            total = near[pl.ds(leaf * p, p)] + dot_t(bs[leaf], leaf_local)
            if leaf == 0:
                total = total + dot(edge_near[0], x_low)
            if leaf == n - 1:
                total = total + dot(edge_near[1], x_high)
            stage[pl.ds(leaf * p, p)] = total.astype(BF)
        if box % 2:
            rows = pl.ds((box - 1) * 2 * p, 4 * p)
            copy = pltpu.make_async_copy(stage.at[rows], out.at[rows], sems.at[box // 2])
            copy.start()
            writes.append(copy)
    for copy in writes:
        copy.wait()


def shifted(array, by):
    peers = lax.axis_size("slab")
    pairs = [(i, i + by) for i in range(peers) if 0 <= i + by < peers]
    return lax.ppermute(array, "slab", pairs)


def body(charges, near_blocks, near_pattern, leaf_basis, transfers, couplings, interactions):
    leaves, panels, rank, rhs = near_blocks.shape[0], near_blocks.shape[2], leaf_basis.shape[1], charges.shape[1]
    plan = Plan(leaves, panels, rank, rhs)
    hbm = pl.BlockSpec(memory_space=pltpu.HBM)
    vmem = pl.BlockSpec(memory_space=pltpu.VMEM)
    smem = pl.BlockSpec(memory_space=pltpu.SMEM)
    chunks = 8
    boxes, trans = couplings.shape[0], transfers.shape[0]

    padded_x, poles, up, down, up2, down2, top, bs, ts = pl.pallas_call(
        lambda *refs: upward_kernel(plan, chunks, *refs),
        in_specs=[hbm, hbm, hbm],
        out_specs=[vmem] * 9,
        out_shape=[
            resident(((leaves + 2) * panels, rhs), BF),
            resident((plan.padded_boxes * rank, rhs), BF),
            resident((plan.msg_rows, rhs), BF),
            resident((plan.msg_rows, rhs), BF),
            resident((2 * rank, rhs), BF),
            resident((2 * rank, rhs), BF),
            resident((rank, rhs), BF),
            resident(leaf_basis.shape, BF),
            resident(transfers.shape, BF),
        ],
        scratch_shapes=[pltpu.SemaphoreType.DMA((chunks + 2,))],
        compiler_params=pltpu.CompilerParams(vmem_limit_bytes=4 * MIB),
        name="upward",
    )(stay(charges), stay(leaf_basis), stay(transfers))

    below, above = shifted(up, 1), shifted(down, -1)
    below2, above2 = shifted(up2, 2), shifted(down2, -2)
    below3, above3 = shifted(top, 3), shifted(top, -3)

    near, local, masked, edge_near = pl.pallas_call(
        lambda *refs: inner_kernel(plan, chunks, *refs),
        in_specs=[smem, smem, vmem, vmem, hbm, hbm],
        out_specs=[vmem] * 4,
        out_shape=[
            resident((leaves * panels, rhs), F32),
            resident((plan.inner_boxes * rank, rhs), F32),
            resident(couplings.shape, BF),
            resident((2, panels, panels), BF),
        ],
        scratch_shapes=[
            pltpu.VMEM(near_blocks.shape, BF),
            pltpu.VMEM(couplings.shape, BF),
            pltpu.SemaphoreType.DMA((chunks + 1,)),
        ],
        cost_estimate=pl.CostEstimate(flops=12_000_000_000, bytes_accessed=16 * MIB, transcendentals=0),
        compiler_params=pltpu.CompilerParams(vmem_limit_bytes=12 * MIB),
        name="inner",
    )(near_pattern.T, interactions.T, keep(padded_x), keep(poles), stay(near_blocks), stay(couplings))

    return pl.pallas_call(
        lambda *refs: final_kernel(plan, *refs),
        in_specs=[vmem] * 12,
        out_specs=hbm,
        out_shape=jax.ShapeDtypeStruct((leaves * panels, rhs), BF),
        scratch_shapes=[
            pltpu.VMEM((rank, rhs), BF),
            pltpu.VMEM((leaves * panels, rhs), BF),
            pltpu.SemaphoreType.DMA((leaves // 4,)),
        ],
        compiler_params=pltpu.CompilerParams(vmem_limit_bytes=12 * MIB),
        name="final",
    )(
        keep(near), keep(local), keep(masked), keep(edge_near), keep(bs), keep(ts),
        keep(below), keep(above), keep(below2), keep(above2), keep(below3), keep(above3),
    )


def solution(mesh):
    spec = ("groups", "slab")
    in_specs = (
        P(spec, None),
        P(spec, None, None, None),
        P(spec, None),
        P(spec, None, None),
        P(spec, None, None),
        P(spec, None, None),
        P(spec, None),
    )
    return jax.shard_map(body, mesh=mesh, in_specs=in_specs, out_specs=P(spec, None), check_vma=False)
```

```python
import jax
import jax.numpy as jnp
from jax import lax
from jax.experimental import pallas as pl
from jax.experimental.pallas import tpu as pltpu
from jax.sharding import PartitionSpec as P

LEVELS = 6
FULL = LEVELS - 2
BF = jnp.bfloat16
F32 = jnp.float32
MIB = 1 << 20


def resident(shape, dtype):
    return pltpu.VMEM(shape, dtype)


def keep(array):
    return pltpu.with_memory_space_constraint(array, pltpu.VMEM)


def stay(array):
    return pltpu.with_memory_space_constraint(array, pltpu.HBM)


def dot(a, b):
    return lax.dot_general(a, b, (((1,), (0,)), ((), ())), preferred_element_type=F32)


class Plan:
    def __init__(self, leaves, panels, rank, rhs):
        self.leaves, self.panels, self.rank, self.rhs = leaves, panels, rank, rhs
        self.count = [leaves >> level for level in range(LEVELS)]
        self.first = [sum(self.count[:level]) for level in range(LEVELS)]
        self.trans = [0] + [sum(self.count[1:level]) for level in range(1, LEVELS)]
        self.padded = [sum(c + 6 for c in self.count[:level]) for level in range(FULL)]
        self.padded_boxes = sum(c + 6 for c in self.count[:FULL])
        self.inner_boxes = sum(self.count[:FULL])
        self.msg_pole = [panels + 2 * rank * level for level in range(FULL)]
        self.msg_small = panels + 2 * rank * FULL
        self.msg_rows = self.msg_small + rank
        self.part_rows = rank * panels // rhs
        self.top_rows = 2 * rank + self.part_rows


def upward_kernel(plan, chunks, charges, basis, transfers, padded_x, poles, up, down, top, bs, ts, sems):
    p, r = plan.panels, plan.rank
    per = plan.leaves // chunks
    copies = []
    for c in range(chunks):
        rows = per * p
        copies.append(
            pltpu.make_async_copy(
                charges.at[pl.ds(c * rows, rows)], padded_x.at[pl.ds(p + c * rows, rows)], sems.at[c]
            )
        )
    basis_copy = pltpu.make_async_copy(basis, bs, sems.at[chunks])
    trans_copy = pltpu.make_async_copy(transfers, ts, sems.at[chunks + 1])
    basis_copy.start()
    copies[0].start()
    trans_copy.start()
    for copy in copies[1:]:
        copy.start()
    padded_x[pl.ds(0, p)] = jnp.zeros((p, plan.rhs), BF)
    padded_x[pl.ds(p * (plan.leaves + 1), p)] = jnp.zeros((p, plan.rhs), BF)
    for level in range(FULL):
        start = plan.padded[level] * r
        poles[pl.ds(start, 3 * r)] = jnp.zeros((3 * r, plan.rhs), BF)
        poles[pl.ds(start + (plan.count[level] + 3) * r, 3 * r)] = jnp.zeros((3 * r, plan.rhs), BF)
    basis_copy.wait()

    def keep(level, box, value):
        n = plan.count[level]
        if level < FULL:
            poles[pl.ds((plan.padded[level] + 3 + box) * r, r)] = value
            if n - 3 <= box <= n - 2:
                up[pl.ds(plan.msg_pole[level] + (box - n + 3) * r, r)] = value
            if 1 <= box <= 2:
                down[pl.ds(plan.msg_pole[level] + (box - 1) * r, r)] = value
        else:
            top[pl.ds(box * r, r)] = value

    def climb(level, box):
        pair = poles[pl.ds((plan.padded[level - 1] + 3 + 2 * box) * r, 2 * r)]
        keep(level, box, dot(ts[plan.trans[level] + box], pair).astype(BF))

    done = [0] * (FULL + 1)

    def climb_ready():
        ready = list(done)
        for level in range(1, FULL + 1):
            while 2 * done[level] + 2 <= ready[level - 1]:
                climb(level, done[level])
                done[level] += 1

    for c in range(chunks):
        copies[c].wait()
        if c == 0:
            trans_copy.wait()
        climb_ready()
        for leaf in range(c * per, (c + 1) * per):
            x = padded_x[pl.ds(p * (leaf + 1), p)]
            keep(0, leaf, dot(bs[leaf], x).astype(BF))
        done[0] = (c + 1) * per
    while done[FULL] < plan.count[FULL]:
        climb_ready()
    for message, leaf, last in ((up, plan.leaves - 1, True), (down, 0, False)):
        message[pl.ds(0, p)] = padded_x[pl.ds(p * (leaf + 1), p)]
        message[pl.ds(plan.msg_small, r), pl.ds(0, p)] = bs[leaf]
        for level in range(1, FULL):
            box = plan.count[level] - 1 if last else 0
            message[pl.ds(plan.msg_small, r), pl.ds(level * p, p)] = ts[plan.trans[level] + box]
    rows = plan.part_rows
    for part in range(plan.rhs // p):
        top[pl.ds(2 * r, rows), pl.ds(part * p, p)] = ts[plan.trans[LEVELS - 1], pl.ds(part * rows, rows)]


def inner_kernel(
    plan, chunks, pattern, flags, padded_x, poles, bs, ts, near_blocks, couplings,
    near, local, masked, edge_near, bs_t, ts_t, nb, sems,
):
    p, r = plan.panels, plan.rank
    per = plan.leaves // chunks
    half = couplings.shape[0] // 2
    coupling_copies = [
        pltpu.make_async_copy(couplings.at[pl.ds(a, n)], masked.at[pl.ds(a, n)], sems.at[chunks + k])
        for k, (a, n) in enumerate(((0, half), (half, couplings.shape[0] - half)))
    ]
    copies = [
        pltpu.make_async_copy(near_blocks.at[pl.ds(c * per, per)], nb.at[pl.ds(c * per, per)], sems.at[c])
        for c in range(chunks)
    ]
    for copy in coupling_copies + copies:
        copy.start()
    for box in range(ts.shape[0]):
        ts_t[box] = ts[box].T
    for leaf in range(bs.shape[0]):
        bs_t[leaf] = bs[leaf].T
    lane = lax.broadcasted_iota(jnp.int32, (r, 4 * r), 1)

    def mask(box):
        low = jnp.where(lane < r, flags[0, box], flags[1, box])
        high = jnp.where(lane < 3 * r, flags[2, box], flags[3, box])
        chosen = jnp.where(lane < 2 * r, low, high)
        value = masked[box] * chosen.astype(F32).astype(BF)
        masked[box] = value
        return value

    def couple(level, box):
        row = (plan.padded[level] + box) * r
        stack = jnp.concatenate([poles[pl.ds(row, 2 * r)], poles[pl.ds(row + 5 * r, 2 * r)]], axis=0)
        index = plan.first[level] + box
        local[pl.ds(index * r, r)] = dot(mask(index), stack)

    for copy in coupling_copies:
        copy.wait()
    for level in range(FULL):
        for box in range(plan.count[level]):
            couple(level, box)
    for box in range(plan.inner_boxes, sum(plan.count)):
        mask(box)

    def side(leaf, slot):
        block = nb[leaf, slot]
        return jnp.where(pattern[slot, leaf] != 0, block, jnp.zeros_like(block))

    def near_one(leaf):
        wide = jnp.concatenate([side(leaf, 0), nb[leaf, 1], side(leaf, 2)], axis=1)
        near[pl.ds(leaf * p, p)] = dot(wide, padded_x[pl.ds(leaf * p, 3 * p)]).astype(BF)

    for c in range(chunks):
        copies[c].wait()
    for leaf in range(plan.leaves):
        near_one(leaf)
    edge_near[0] = side(0, 0)
    edge_near[1] = side(plan.leaves - 1, 2)


def top_kernel(plan, peers, gathered, local, masked, ts, ts_t, third, held, sems):
    r, p = plan.rank, plan.panels
    me = lax.axis_index("slab")
    copies = {}
    for k, by in enumerate((-3, -2, -1, 1, 2, 3)):
        source = jnp.clip(me + by, 0, peers - 1)
        copies[by] = pltpu.make_async_copy(gathered.at[source], held.at[k], sems.at[k])
        copies[by].start()
    pair, fifth = {}, {}
    for k, by in enumerate((-3, -2, -1, 1, 2, 3)):
        copies[by].wait()
        inside = (me + by >= 0) if by < 0 else (me + by < peers)
        value = held[k, pl.ds(0, 2 * r)]
        pair[by] = jnp.where(inside, value, jnp.zeros_like(value))
        if abs(by) > 1:
            rows = plan.part_rows
            matrix = jnp.concatenate(
                [held[k, pl.ds(2 * r, rows), pl.ds(part * p, p)] for part in range(plan.rhs // p)], axis=0
            )
            fifth[by] = dot(matrix, pair[by]).astype(BF)
    box = plan.first[LEVELS - 1]
    stack = jnp.concatenate([fifth[-3], fifth[-2], fifth[2], fifth[3]], axis=0)
    summit = dot(masked[box], stack).astype(BF)
    pushed = dot(ts_t[plan.trans[LEVELS - 1]], summit)
    stacks = (
        [pair[-2][r:], pair[-1][:r], pair[1]],
        [pair[-1], pair[1][r:], pair[2][:r]],
    )
    for k, stack in enumerate(stacks):
        gained = dot(masked[plan.first[FULL] + k], jnp.concatenate(stack, axis=0))
        value = (gained + pushed[k * r : (k + 1) * r]).astype(BF)
        index = (plan.first[FULL - 1] + 2 * k) * r
        third[pl.ds(2 * k * r, 2 * r)] = local[pl.ds(index, 2 * r)] + dot(ts_t[plan.trans[FULL] + k], value)


def final_kernel(plan, near, local, third, masked, edge_near, bs_t, ts_t, below, above, out, stage, sems):
    p, r, n = plan.panels, plan.rank, plan.leaves

    def edges(message, last):
        x = message[pl.ds(0, p)]
        small = pl.ds(plan.msg_small, r)
        rim = [dot(message[small, pl.ds(0, p)], x).astype(BF)]
        sent = [message[pl.ds(plan.msg_pole[level], 2 * r)] for level in range(FULL)]
        for level in range(1, FULL):
            if last:
                pair = jnp.concatenate([sent[level - 1][r:], rim[-1]], axis=0)
            else:
                pair = jnp.concatenate([rim[-1], sent[level - 1][:r]], axis=0)
            rim.append(dot(message[small, pl.ds(level * p, p)], pair).astype(BF))
        return x, rim, sent

    x_low, rim_low, sent_low = edges(below, True)
    x_high, rim_high, sent_high = edges(above, False)

    rims = []
    for level in range(FULL):
        first, m = plan.first[level], plan.count[level]
        low = jnp.concatenate([sent_low[level], rim_low[level]], axis=0)
        high = jnp.concatenate([rim_high[level], sent_high[level]], axis=0)
        gain = [
            (0, dot(masked[first, :, pl.ds(0, 2 * r)], low[: 2 * r])),
            (1, dot(masked[first + 1, :, pl.ds(0, 2 * r)], low[r:])),
            (2, dot(masked[first + 2, :, pl.ds(0, r)], low[2 * r :])),
            (m - 1, dot(masked[first + m - 1, :, pl.ds(2 * r, 2 * r)], high[r:])),
            (m - 2, dot(masked[first + m - 2, :, pl.ds(2 * r, 2 * r)], high[: 2 * r])),
            (m - 3, dot(masked[first + m - 3, :, pl.ds(3 * r, r)], high[:r])),
        ]
        sums = {}
        for place, value in gain:
            sums[place] = sums[place] + value if place in sums else value
        rims.append(sums)

    def settled(level, box, value):
        if box in rims[level]:
            value = value + rims[level][box]
        return value.astype(BF)

    current = [settled(FULL - 1, box, third[pl.ds(box * r, r)]) for box in range(plan.count[FULL - 1])]
    for level in range(FULL - 1, 1, -1):
        lower = []
        for box, value in enumerate(current):
            push = dot(ts_t[plan.trans[level] + box], value)
            for k in range(2):
                index = (plan.first[level - 1] + 2 * box + k) * r
                lower.append(settled(level - 1, 2 * box + k, local[pl.ds(index, r)] + push[k * r : (k + 1) * r]))
        current = lower

    writes = []
    for box, value in enumerate(current):
        push = dot(ts_t[plan.trans[1] + box], value)
        for k in range(2):
            leaf = 2 * box + k
            leaf_local = settled(0, leaf, local[pl.ds(leaf * r, r)] + push[k * r : (k + 1) * r])
            total = near[pl.ds(leaf * p, p)].astype(F32) + dot(bs_t[leaf], leaf_local)
            if leaf == 0:
                total = total + dot(edge_near[0], x_low)
            if leaf == n - 1:
                total = total + dot(edge_near[1], x_high)
            stage[pl.ds(leaf * p, p)] = total.astype(BF)
        if box % 2:
            rows = pl.ds((box - 1) * 2 * p, 4 * p)
            copy = pltpu.make_async_copy(stage.at[rows], out.at[rows], sems.at[box // 2])
            copy.start()
            writes.append(copy)
    for copy in writes:
        copy.wait()


def shifted(array, by):
    peers = lax.axis_size("slab")
    pairs = [(i, i + by) for i in range(peers) if 0 <= i + by < peers]
    return lax.ppermute(array, "slab", pairs)


def body(charges, near_blocks, near_pattern, leaf_basis, transfers, couplings, interactions):
    leaves, panels, rank, rhs = near_blocks.shape[0], near_blocks.shape[2], leaf_basis.shape[1], charges.shape[1]
    plan = Plan(leaves, panels, rank, rhs)
    hbm = pl.BlockSpec(memory_space=pltpu.HBM)
    vmem = pl.BlockSpec(memory_space=pltpu.VMEM)
    smem = pl.BlockSpec(memory_space=pltpu.SMEM)
    chunks = 8

    padded_x, poles, up, down, top, bs, ts = pl.pallas_call(
        lambda *refs: upward_kernel(plan, chunks, *refs),
        in_specs=[hbm, hbm, hbm],
        out_specs=[vmem] * 7,
        out_shape=[
            resident(((leaves + 2) * panels, rhs), BF),
            resident((plan.padded_boxes * rank, rhs), BF),
            resident((plan.msg_rows, rhs), BF),
            resident((plan.msg_rows, rhs), BF),
            resident((plan.top_rows, rhs), BF),
            resident(leaf_basis.shape, BF),
            resident(transfers.shape, BF),
        ],
        scratch_shapes=[pltpu.SemaphoreType.DMA((chunks + 2,))],
        compiler_params=pltpu.CompilerParams(vmem_limit_bytes=6 * MIB),
        name="upward",
    )(stay(charges), stay(leaf_basis), stay(transfers))

    gathered = lax.all_gather(top, "slab")
    below, above = shifted(up, 1), shifted(down, -1)

    near, local, masked, edge_near, bs_t, ts_t = pl.pallas_call(
        lambda *refs: inner_kernel(plan, 4, *refs),
        in_specs=[smem, smem, vmem, vmem, vmem, vmem, hbm, hbm],
        out_specs=[vmem] * 6,
        out_shape=[
            resident((leaves * panels, rhs), BF),
            resident((plan.inner_boxes * rank, rhs), F32),
            resident(couplings.shape, BF),
            resident((2, panels, panels), BF),
            resident((leaves, panels, rank), BF),
            resident((transfers.shape[0], panels, rank), BF),
        ],
        scratch_shapes=[
            pltpu.VMEM(near_blocks.shape, BF),
            pltpu.SemaphoreType.DMA((6,)),
        ],
        compiler_params=pltpu.CompilerParams(vmem_limit_bytes=12 * MIB),
        cost_estimate=pl.CostEstimate(flops=12_000_000_000, bytes_accessed=16 * MIB, transcendentals=0),
        name="inner",
    )(
        near_pattern.T, interactions.T, keep(padded_x), keep(poles), keep(bs), keep(ts),
        stay(near_blocks), stay(couplings),
    )

    third = pl.pallas_call(
        lambda *refs: top_kernel(plan, gathered.shape[0], *refs),
        in_specs=[hbm, vmem, vmem, vmem, vmem],
        out_specs=vmem,
        out_shape=resident((plan.count[FULL - 1] * rank, rhs), F32),
        scratch_shapes=[
            pltpu.VMEM((6, plan.top_rows, rhs), BF),
            pltpu.SemaphoreType.DMA((6,)),
        ],
        compiler_params=pltpu.CompilerParams(vmem_limit_bytes=6 * MIB),
        name="top",
    )(stay(gathered), keep(local), keep(masked), keep(ts), keep(ts_t))

    return pl.pallas_call(
        lambda *refs: final_kernel(plan, *refs),
        in_specs=[vmem] * 9,
        out_specs=hbm,
        out_shape=jax.ShapeDtypeStruct((leaves * panels, rhs), BF),
        scratch_shapes=[
            pltpu.VMEM((leaves * panels, rhs), BF),
            pltpu.SemaphoreType.DMA((leaves // 4,)),
        ],
        compiler_params=pltpu.CompilerParams(vmem_limit_bytes=12 * MIB),
        name="final",
    )(
        keep(near), keep(local), keep(third), keep(masked), keep(edge_near), keep(bs_t), keep(ts_t),
        keep(below), keep(above),
    )


def solution(mesh):
    spec = ("groups", "slab")
    in_specs = (
        P(spec, None),
        P(spec, None, None, None),
        P(spec, None),
        P(spec, None, None),
        P(spec, None, None),
        P(spec, None, None),
        P(spec, None),
    )
    return jax.shard_map(body, mesh=mesh, in_specs=in_specs, out_specs=P(spec, None), check_vma=False)
```

```python
import jax
import jax.numpy as jnp
from jax import lax
from jax.experimental import pallas as pl
from jax.experimental.pallas import tpu as pltpu
from jax.sharding import PartitionSpec as P

LEVELS = 6
FULL = LEVELS - 2
BF = jnp.bfloat16
F32 = jnp.float32
MIB = 1 << 20


def resident(shape, dtype):
    return pltpu.VMEM(shape, dtype)


def keep(array):
    return pltpu.with_memory_space_constraint(array, pltpu.VMEM)


def stay(array):
    return pltpu.with_memory_space_constraint(array, pltpu.HBM)


def dot(a, b):
    return lax.dot_general(a, b, (((1,), (0,)), ((), ())), preferred_element_type=F32)


class Plan:
    def __init__(self, leaves, panels, rank, rhs):
        self.leaves, self.panels, self.rank, self.rhs = leaves, panels, rank, rhs
        self.count = [leaves >> level for level in range(LEVELS)]
        self.first = [sum(self.count[:level]) for level in range(LEVELS)]
        self.trans = [0] + [sum(self.count[1:level]) for level in range(1, LEVELS)]
        self.padded = [sum(c + 6 for c in self.count[:level]) for level in range(FULL)]
        self.padded_boxes = sum(c + 6 for c in self.count[:FULL])
        self.inner_boxes = sum(self.count[:FULL])
        self.msg_pole = [panels + 2 * rank * level for level in range(FULL)]
        self.msg_top = panels + 2 * rank * FULL
        self.msg_small = self.msg_top + rank
        self.msg_last = self.msg_small + rank
        self.part_rows = rank * panels // rhs
        self.msg_rows = self.msg_last + self.part_rows


def upward_kernel(plan, chunks, charges, basis, transfers, padded_x, poles, up, down, up2, down2, top, bs, ts, pair4, sems):
    p, r = plan.panels, plan.rank
    per = plan.leaves // chunks
    copies = []
    for c in range(chunks):
        rows = per * p
        copies.append(
            pltpu.make_async_copy(
                charges.at[pl.ds(c * rows, rows)], padded_x.at[pl.ds(p + c * rows, rows)], sems.at[c]
            )
        )
    basis_copy = pltpu.make_async_copy(basis, bs, sems.at[chunks])
    trans_copy = pltpu.make_async_copy(transfers, ts, sems.at[chunks + 1])
    basis_copy.start()
    copies[0].start()
    trans_copy.start()
    for copy in copies[1:]:
        copy.start()
    padded_x[pl.ds(0, p)] = jnp.zeros((p, plan.rhs), BF)
    padded_x[pl.ds(p * (plan.leaves + 1), p)] = jnp.zeros((p, plan.rhs), BF)
    for level in range(FULL):
        start = plan.padded[level] * r
        poles[pl.ds(start, 3 * r)] = jnp.zeros((3 * r, plan.rhs), BF)
        poles[pl.ds(start + (plan.count[level] + 3) * r, 3 * r)] = jnp.zeros((3 * r, plan.rhs), BF)
    basis_copy.wait()

    def keep(level, box, value):
        n = plan.count[level]
        if level < FULL:
            poles[pl.ds((plan.padded[level] + 3 + box) * r, r)] = value
            if n - 3 <= box <= n - 2:
                up[pl.ds(plan.msg_pole[level] + (box - n + 3) * r, r)] = value
            if 1 <= box <= 2:
                down[pl.ds(plan.msg_pole[level] + (box - 1) * r, r)] = value
        elif level == FULL:
            (up if box == 0 else down)[pl.ds(plan.msg_top, r)] = value
            (down2 if box == 0 else up2)[pl.ds(0, r)] = value
            pair4[pl.ds(box * r, r)] = value
        else:
            for message in (up2, down2):
                message[pl.ds(r, r)] = value
            top[...] = value

    def climb(level, box):
        if level <= FULL:
            pair = poles[pl.ds((plan.padded[level - 1] + 3 + 2 * box) * r, 2 * r)]
        else:
            pair = pair4[...]
        keep(level, box, dot(ts[plan.trans[level] + box], pair).astype(BF))

    done = [0] * LEVELS

    def climb_ready():
        ready = list(done)
        for level in range(1, LEVELS):
            while 2 * done[level] + 2 <= ready[level - 1]:
                climb(level, done[level])
                done[level] += 1

    for c in range(chunks):
        copies[c].wait()
        if c == 0:
            trans_copy.wait()
        climb_ready()
        for leaf in range(c * per, (c + 1) * per):
            x = padded_x[pl.ds(p * (leaf + 1), p)]
            keep(0, leaf, dot(bs[leaf], x).astype(BF))
        done[0] = (c + 1) * per
    while done[LEVELS - 1] < plan.count[LEVELS - 1]:
        climb_ready()
    for message, leaf, last in ((up, plan.leaves - 1, True), (down, 0, False)):
        message[pl.ds(0, p)] = padded_x[pl.ds(p * (leaf + 1), p)]
        message[pl.ds(plan.msg_small, r), pl.ds(0, p)] = bs[leaf]
        for level in range(1, FULL):
            box = plan.count[level] - 1 if last else 0
            message[pl.ds(plan.msg_small, r), pl.ds(level * p, p)] = ts[plan.trans[level] + box]
        matrix = plan.trans[FULL] + (plan.count[FULL] - 1 if last else 0)
        rows = plan.part_rows
        for part in range(plan.rhs // p):
            message[pl.ds(plan.msg_last, rows), pl.ds(part * p, p)] = ts[matrix, pl.ds(part * rows, rows)]


def inner_kernel(
    plan, chunks, pattern, flags, padded_x, poles, bs, ts, near_blocks, couplings,
    near, local, masked, edge_near, bs_t, ts_t, nb, sems,
):
    p, r = plan.panels, plan.rank
    per = plan.leaves // chunks
    half = couplings.shape[0] // 2
    coupling_copies = [
        pltpu.make_async_copy(couplings.at[pl.ds(a, n)], masked.at[pl.ds(a, n)], sems.at[chunks + k])
        for k, (a, n) in enumerate(((0, half), (half, couplings.shape[0] - half)))
    ]
    copies = [
        pltpu.make_async_copy(near_blocks.at[pl.ds(c * per, per)], nb.at[pl.ds(c * per, per)], sems.at[c])
        for c in range(chunks)
    ]
    for copy in coupling_copies + copies:
        copy.start()
    for box in range(ts.shape[0]):
        ts_t[box] = ts[box].T
    for leaf in range(bs.shape[0]):
        bs_t[leaf] = bs[leaf].T
    lane = lax.broadcasted_iota(jnp.int32, (r, 4 * r), 1)

    def mask(box):
        low = jnp.where(lane < r, flags[0, box], flags[1, box])
        high = jnp.where(lane < 3 * r, flags[2, box], flags[3, box])
        chosen = jnp.where(lane < 2 * r, low, high)
        value = masked[box] * chosen.astype(F32).astype(BF)
        masked[box] = value
        return value

    def couple(level, box):
        row = (plan.padded[level] + box) * r
        stack = jnp.concatenate([poles[pl.ds(row, 2 * r)], poles[pl.ds(row + 5 * r, 2 * r)]], axis=0)
        index = plan.first[level] + box
        local[pl.ds(index * r, r)] = dot(mask(index), stack)

    for copy in coupling_copies:
        copy.wait()
    for level in range(FULL):
        for box in range(plan.count[level]):
            couple(level, box)
    for box in range(plan.inner_boxes, sum(plan.count)):
        mask(box)

    def side(leaf, slot):
        block = nb[leaf, slot]
        return jnp.where(pattern[slot, leaf] != 0, block, jnp.zeros_like(block))

    def near_one(leaf):
        wide = jnp.concatenate([side(leaf, 0), nb[leaf, 1], side(leaf, 2)], axis=1)
        near[pl.ds(leaf * p, p)] = dot(wide, padded_x[pl.ds(leaf * p, 3 * p)]).astype(BF)

    for c in range(chunks):
        copies[c].wait()
    for leaf in range(plan.leaves):
        near_one(leaf)
    edge_near[0] = side(0, 0)
    edge_near[1] = side(plan.leaves - 1, 2)


def final_kernel(
    plan, near, local, masked, edge_near, bs_t, ts_t, below, above, below2, above2, below3, above3,
    out, loc, stage, sems,
):
    p, r, n = plan.panels, plan.rank, plan.leaves
    small = pl.ds(plan.msg_small, r)
    messages = (below, above)

    sent = [[message[pl.ds(plan.msg_pole[level], 2 * r)] for level in range(FULL)] for message in messages]
    rim = [[dot(message[small, pl.ds(0, p)], message[pl.ds(0, p)]).astype(BF)] for message in messages]
    for level in range(1, FULL + 1):
        for k, message in enumerate(messages):
            if level < FULL:
                matrix = message[small, pl.ds(level * p, p)]
            else:
                rows = pl.ds(plan.msg_last, plan.part_rows)
                matrix = jnp.concatenate([message[rows, pl.ds(part * p, p)] for part in range(plan.rhs // p)], axis=0)
            children = [sent[k][level - 1][r:], rim[k][-1]] if k == 0 else [rim[k][-1], sent[k][level - 1][:r]]
            rim[k].append(dot(matrix, jnp.concatenate(children, axis=0)).astype(BF))

    def place(level, box):
        return pl.ds((plan.first[level] + box) * r, r)

    stack = jnp.concatenate([below3[...], below2[pl.ds(r, r)], above2[pl.ds(r, r)], above3[...]], axis=0)
    summit = dot(masked[plan.first[LEVELS - 1]], stack).astype(BF)
    pushed = dot(ts_t[plan.trans[LEVELS - 1]], summit)
    low, high = below[pl.ds(plan.msg_top, r)], above[pl.ds(plan.msg_top, r)]
    stacks = ([below2[pl.ds(0, r)], low, rim[1][FULL], high], [low, rim[0][FULL], high, above2[pl.ds(0, r)]])
    for k, stack in enumerate(stacks):
        gained = dot(masked[plan.first[FULL] + k], jnp.concatenate(stack, axis=0))
        loc[place(FULL, k)] = (gained + pushed[k * r : (k + 1) * r]).astype(BF)

    def rim_gain(level, box):
        first, m = plan.first[level], plan.count[level]
        low = [sent[0][level][:r], sent[0][level][r:], rim[0][level]]
        high = [rim[1][level], sent[1][level][:r], sent[1][level][r:]]
        gain = None
        if box < 3:
            used = low[box : box + 2]
            gain = dot(masked[first + box, :, pl.ds(0, len(used) * r)], jnp.concatenate(used, axis=0))
        if box >= m - 3:
            from_end = box - (m - 3)
            used = high[max(from_end - 1, 0) : from_end + 1]
            start = (4 - len(used)) * r if from_end == 0 else 2 * r
            value = dot(masked[first + box, :, pl.ds(start, len(used) * r)], jnp.concatenate(used, axis=0))
            gain = value if gain is None else gain + value
        return gain

    for level in range(FULL, 0, -1):
        for box in range(plan.count[level]):
            push = dot(ts_t[plan.trans[level] + box], loc[place(level, box)])
            for k in range(2):
                child = 2 * box + k
                value = local[place(level - 1, child)] + push[k * r : (k + 1) * r]
                gain = rim_gain(level - 1, child)
                loc[place(level - 1, child)] = (value if gain is None else value + gain).astype(BF)

    writes = []
    per = n // sems.shape[0]
    for leaf in range(n):
        total = near[pl.ds(leaf * p, p)].astype(F32) + dot(bs_t[leaf], loc[place(0, leaf)])
        if leaf == 0:
            total = total + dot(edge_near[0], below[pl.ds(0, p)])
        if leaf == n - 1:
            total = total + dot(edge_near[1], above[pl.ds(0, p)])
        stage[pl.ds(leaf * p, p)] = total.astype(BF)
        if (leaf + 1) % per == 0:
            rows = pl.ds((leaf + 1 - per) * p, per * p)
            copy = pltpu.make_async_copy(stage.at[rows], out.at[rows], sems.at[leaf // per])
            copy.start()
            writes.append(copy)
    for copy in writes:
        copy.wait()


def shifted(array, by):
    peers = lax.axis_size("slab")
    pairs = [(i, i + by) for i in range(peers) if 0 <= i + by < peers]
    return lax.ppermute(array, "slab", pairs)


def body(charges, near_blocks, near_pattern, leaf_basis, transfers, couplings, interactions):
    leaves, panels, rank, rhs = near_blocks.shape[0], near_blocks.shape[2], leaf_basis.shape[1], charges.shape[1]
    plan = Plan(leaves, panels, rank, rhs)
    hbm = pl.BlockSpec(memory_space=pltpu.HBM)
    vmem = pl.BlockSpec(memory_space=pltpu.VMEM)
    smem = pl.BlockSpec(memory_space=pltpu.SMEM)
    chunks = 8

    padded_x, poles, up, down, up2, down2, top, bs, ts = pl.pallas_call(
        lambda *refs: upward_kernel(plan, chunks, *refs),
        in_specs=[hbm, hbm, hbm],
        out_specs=[vmem] * 9,
        out_shape=[
            resident(((leaves + 2) * panels, rhs), BF),
            resident((plan.padded_boxes * rank, rhs), BF),
            resident((plan.msg_rows, rhs), BF),
            resident((plan.msg_rows, rhs), BF),
            resident((2 * rank, rhs), BF),
            resident((2 * rank, rhs), BF),
            resident((rank, rhs), BF),
            resident(leaf_basis.shape, BF),
            resident(transfers.shape, BF),
        ],
        scratch_shapes=[pltpu.VMEM((2 * rank, rhs), BF), pltpu.SemaphoreType.DMA((chunks + 2,))],
        compiler_params=pltpu.CompilerParams(vmem_limit_bytes=6 * MIB),
        name="upward",
    )(stay(charges), stay(leaf_basis), stay(transfers))

    below, above = shifted(up, 1), shifted(down, -1)
    below2, above2 = shifted(up2, 2), shifted(down2, -2)
    below3, above3 = shifted(top, 3), shifted(top, -3)

    near, local, masked, edge_near, bs_t, ts_t = pl.pallas_call(
        lambda *refs: inner_kernel(plan, 4, *refs),
        in_specs=[smem, smem, vmem, vmem, vmem, vmem, hbm, hbm],
        out_specs=[vmem] * 6,
        out_shape=[
            resident((leaves * panels, rhs), BF),
            resident((plan.inner_boxes * rank, rhs), F32),
            resident(couplings.shape, BF),
            resident((2, panels, panels), BF),
            resident((leaves, panels, rank), BF),
            resident((transfers.shape[0], panels, rank), BF),
        ],
        scratch_shapes=[
            pltpu.VMEM(near_blocks.shape, BF),
            pltpu.SemaphoreType.DMA((6,)),
        ],
        compiler_params=pltpu.CompilerParams(vmem_limit_bytes=12 * MIB),
        cost_estimate=pl.CostEstimate(flops=12_000_000_000, bytes_accessed=16 * MIB, transcendentals=0),
        name="inner",
    )(
        near_pattern.T, interactions.T, keep(padded_x), keep(poles), keep(bs), keep(ts),
        stay(near_blocks), stay(couplings),
    )

    return pl.pallas_call(
        lambda *refs: final_kernel(plan, *refs),
        in_specs=[vmem] * 12,
        out_specs=hbm,
        out_shape=jax.ShapeDtypeStruct((leaves * panels, rhs), BF),
        scratch_shapes=[
            pltpu.VMEM((couplings.shape[0] * rank, rhs), BF),
            pltpu.VMEM((leaves * panels, rhs), BF),
            pltpu.SemaphoreType.DMA((leaves // 4,)),
        ],
        compiler_params=pltpu.CompilerParams(vmem_limit_bytes=14 * MIB),
        name="final",
    )(
        keep(near), keep(local), keep(masked), keep(edge_near), keep(bs_t), keep(ts_t),
        keep(below), keep(above), keep(below2), keep(above2), keep(below3), keep(above3),
    )


def solution(mesh):
    spec = ("groups", "slab")
    in_specs = (
        P(spec, None),
        P(spec, None, None, None),
        P(spec, None),
        P(spec, None, None),
        P(spec, None, None),
        P(spec, None, None),
        P(spec, None),
    )
    return jax.shard_map(body, mesh=mesh, in_specs=in_specs, out_specs=P(spec, None), check_vma=False)
```

```python
import jax
import jax.numpy as jnp
from jax import lax
from jax.experimental import pallas as pl
from jax.experimental.pallas import tpu as pltpu
from jax.sharding import PartitionSpec as P

LEVELS = 6
FULL = LEVELS - 2
BF = jnp.bfloat16
F32 = jnp.float32
MIB = 1 << 20


def resident(shape, dtype):
    return pltpu.VMEM(shape, dtype)


def keep(array):
    return pltpu.with_memory_space_constraint(array, pltpu.VMEM)


def stay(array):
    return pltpu.with_memory_space_constraint(array, pltpu.HBM)


def dot(a, b):
    return lax.dot_general(a, b, (((1,), (0,)), ((), ())), preferred_element_type=F32)


class Plan:
    def __init__(self, leaves, panels, rank, rhs):
        self.leaves, self.panels, self.rank, self.rhs = leaves, panels, rank, rhs
        self.count = [leaves >> level for level in range(LEVELS)]
        self.first = [sum(self.count[:level]) for level in range(LEVELS)]
        self.trans = [0] + [sum(self.count[1:level]) for level in range(1, LEVELS)]
        self.padded = [sum(c + 6 for c in self.count[:level]) for level in range(FULL)]
        self.padded_boxes = sum(c + 6 for c in self.count[:FULL])
        self.inner_boxes = sum(self.count[:FULL])
        self.msg_pole = [panels + 2 * rank * level for level in range(FULL)]
        self.msg_top = panels + 2 * rank * FULL
        self.msg_small = self.msg_top + rank
        self.msg_last = self.msg_small + rank
        self.part_rows = rank * panels // rhs
        self.msg_rows = self.msg_last + self.part_rows


def upward_kernel(plan, chunks, charges, basis, transfers, padded_x, poles, up, down, top, pair4, bs, ts, sems):
    p, r = plan.panels, plan.rank
    per = plan.leaves // chunks
    copies = []
    for c in range(chunks):
        rows = per * p
        copies.append(
            pltpu.make_async_copy(
                charges.at[pl.ds(c * rows, rows)], padded_x.at[pl.ds(p + c * rows, rows)], sems.at[c]
            )
        )
    basis_copy = pltpu.make_async_copy(basis, bs, sems.at[chunks])
    trans_copy = pltpu.make_async_copy(transfers, ts, sems.at[chunks + 1])
    basis_copy.start()
    copies[0].start()
    trans_copy.start()
    for copy in copies[1:]:
        copy.start()
    padded_x[pl.ds(0, p)] = jnp.zeros((p, plan.rhs), BF)
    padded_x[pl.ds(p * (plan.leaves + 1), p)] = jnp.zeros((p, plan.rhs), BF)
    for level in range(FULL):
        start = plan.padded[level] * r
        poles[pl.ds(start, 3 * r)] = jnp.zeros((3 * r, plan.rhs), BF)
        poles[pl.ds(start + (plan.count[level] + 3) * r, 3 * r)] = jnp.zeros((3 * r, plan.rhs), BF)
    basis_copy.wait()

    def keep(level, box, value):
        n = plan.count[level]
        if level < FULL:
            poles[pl.ds((plan.padded[level] + 3 + box) * r, r)] = value
            if n - 3 <= box <= n - 2:
                up[pl.ds(plan.msg_pole[level] + (box - n + 3) * r, r)] = value
            if 1 <= box <= 2:
                down[pl.ds(plan.msg_pole[level] + (box - 1) * r, r)] = value
        elif level == FULL:
            (up if box == 0 else down)[pl.ds(plan.msg_top, r)] = value
            pair4[pl.ds(box * r, r)] = value
        else:
            top[...] = value

    def climb(level, box):
        if level <= FULL:
            pair = poles[pl.ds((plan.padded[level - 1] + 3 + 2 * box) * r, 2 * r)]
        else:
            pair = pair4[...]
        keep(level, box, dot(ts[plan.trans[level] + box], pair).astype(BF))

    done = [0] * LEVELS

    def climb_ready():
        ready = list(done)
        for level in range(1, LEVELS):
            while 2 * done[level] + 2 <= ready[level - 1]:
                climb(level, done[level])
                done[level] += 1

    for c in range(chunks):
        copies[c].wait()
        if c == 0:
            trans_copy.wait()
        climb_ready()
        for leaf in range(c * per, (c + 1) * per):
            x = padded_x[pl.ds(p * (leaf + 1), p)]
            keep(0, leaf, dot(bs[leaf], x).astype(BF))
        done[0] = (c + 1) * per
    while done[LEVELS - 1] < plan.count[LEVELS - 1]:
        climb_ready()
    for message, leaf, last in ((up, plan.leaves - 1, True), (down, 0, False)):
        message[pl.ds(0, p)] = padded_x[pl.ds(p * (leaf + 1), p)]
        message[pl.ds(plan.msg_small, r), pl.ds(0, p)] = bs[leaf]
        for level in range(1, FULL):
            box = plan.count[level] - 1 if last else 0
            message[pl.ds(plan.msg_small, r), pl.ds(level * p, p)] = ts[plan.trans[level] + box]
        matrix = plan.trans[FULL] + (plan.count[FULL] - 1 if last else 0)
        rows = plan.part_rows
        for part in range(plan.rhs // p):
            message[pl.ds(plan.msg_last, rows), pl.ds(part * p, p)] = ts[matrix, pl.ds(part * rows, rows)]


def couple_kernel(
    plan, flags, poles, bs, ts, top, pair_top, couplings,
    local, masked, bs_t, ts_t, up2, down2, top_out, sems,
):
    p, r = plan.panels, plan.rank
    half = couplings.shape[0] // 2
    copies = [
        pltpu.make_async_copy(couplings.at[pl.ds(a, n)], masked.at[pl.ds(a, n)], sems.at[k])
        for k, (a, n) in enumerate(((0, half), (half, couplings.shape[0] - half)))
    ]
    for copy in copies:
        copy.start()
    up2[pl.ds(0, r)] = pair_top[pl.ds(r, r)]
    down2[pl.ds(0, r)] = pair_top[pl.ds(0, r)]
    for message in (up2, down2):
        message[pl.ds(r, r)] = top[...]
    top_out[...] = top[...]
    for box in range(ts.shape[0]):
        ts_t[box] = ts[box].T
    for leaf in range(bs.shape[0]):
        bs_t[leaf] = bs[leaf].T
    lane = lax.broadcasted_iota(jnp.int32, (r, 4 * r), 1)

    def mask(box):
        low = jnp.where(lane < r, flags[0, box], flags[1, box])
        high = jnp.where(lane < 3 * r, flags[2, box], flags[3, box])
        chosen = jnp.where(lane < 2 * r, low, high)
        value = masked[box] * chosen.astype(F32).astype(BF)
        masked[box] = value
        return value

    for copy in copies:
        copy.wait()
    for level in range(FULL):
        for box in range(plan.count[level]):
            row = (plan.padded[level] + box) * r
            stack = jnp.concatenate([poles[pl.ds(row, 2 * r)], poles[pl.ds(row + 5 * r, 2 * r)]], axis=0)
            index = plan.first[level] + box
            local[pl.ds(index * r, r)] = dot(mask(index), stack)
    for box in range(plan.inner_boxes, sum(plan.count)):
        mask(box)


def near_kernel(plan, chunks, pattern, padded_x, near_blocks, near, edge_near, nb, sems):
    p = plan.panels
    per = plan.leaves // chunks
    copies = [
        pltpu.make_async_copy(near_blocks.at[pl.ds(c * per, per)], nb.at[pl.ds(c * per, per)], sems.at[c])
        for c in range(chunks)
    ]
    for copy in copies:
        copy.start()

    def side(leaf, slot):
        block = nb[leaf, slot]
        return jnp.where(pattern[slot, leaf] != 0, block, jnp.zeros_like(block))

    for c in range(chunks):
        copies[c].wait()
        for leaf in range(c * per, (c + 1) * per):
            wide = jnp.concatenate([side(leaf, 0), nb[leaf, 1], side(leaf, 2)], axis=1)
            near[pl.ds(leaf * p, p)] = dot(wide, padded_x[pl.ds(leaf * p, 3 * p)]).astype(BF)
    edge_near[0] = side(0, 0)
    edge_near[1] = side(plan.leaves - 1, 2)


def final_kernel(
    plan, near, local, masked, edge_near, bs_t, ts_t, below, above, below2, above2, below3, above3,
    out, loc, stage, sems,
):
    p, r, n = plan.panels, plan.rank, plan.leaves
    small = pl.ds(plan.msg_small, r)
    messages = (below, above)

    sent = [[message[pl.ds(plan.msg_pole[level], 2 * r)] for level in range(FULL)] for message in messages]
    rim = [[dot(message[small, pl.ds(0, p)], message[pl.ds(0, p)]).astype(BF)] for message in messages]
    for level in range(1, FULL + 1):
        for k, message in enumerate(messages):
            if level < FULL:
                matrix = message[small, pl.ds(level * p, p)]
            else:
                rows = pl.ds(plan.msg_last, plan.part_rows)
                matrix = jnp.concatenate([message[rows, pl.ds(part * p, p)] for part in range(plan.rhs // p)], axis=0)
            children = [sent[k][level - 1][r:], rim[k][-1]] if k == 0 else [rim[k][-1], sent[k][level - 1][:r]]
            rim[k].append(dot(matrix, jnp.concatenate(children, axis=0)).astype(BF))

    def place(level, box):
        return pl.ds((plan.first[level] + box) * r, r)

    stack = jnp.concatenate([below3[...], below2[pl.ds(r, r)], above2[pl.ds(r, r)], above3[...]], axis=0)
    summit = dot(masked[plan.first[LEVELS - 1]], stack).astype(BF)
    pushed = dot(ts_t[plan.trans[LEVELS - 1]], summit)
    low, high = below[pl.ds(plan.msg_top, r)], above[pl.ds(plan.msg_top, r)]
    stacks = ([below2[pl.ds(0, r)], low, rim[1][FULL], high], [low, rim[0][FULL], high, above2[pl.ds(0, r)]])
    for k, stack in enumerate(stacks):
        gained = dot(masked[plan.first[FULL] + k], jnp.concatenate(stack, axis=0))
        loc[place(FULL, k)] = (gained + pushed[k * r : (k + 1) * r]).astype(BF)

    def rim_gain(level, box):
        first, m = plan.first[level], plan.count[level]
        low = [sent[0][level][:r], sent[0][level][r:], rim[0][level]]
        high = [rim[1][level], sent[1][level][:r], sent[1][level][r:]]
        gain = None
        if box < 3:
            used = low[box : box + 2]
            gain = dot(masked[first + box, :, pl.ds(0, len(used) * r)], jnp.concatenate(used, axis=0))
        if box >= m - 3:
            from_end = box - (m - 3)
            used = high[max(from_end - 1, 0) : from_end + 1]
            start = (4 - len(used)) * r if from_end == 0 else 2 * r
            value = dot(masked[first + box, :, pl.ds(start, len(used) * r)], jnp.concatenate(used, axis=0))
            gain = value if gain is None else gain + value
        return gain

    for level in range(FULL, 0, -1):
        for box in range(plan.count[level]):
            push = dot(ts_t[plan.trans[level] + box], loc[place(level, box)])
            for k in range(2):
                child = 2 * box + k
                value = local[place(level - 1, child)] + push[k * r : (k + 1) * r]
                gain = rim_gain(level - 1, child)
                loc[place(level - 1, child)] = (value if gain is None else value + gain).astype(BF)

    writes = []
    per = n // sems.shape[0]
    for leaf in range(n):
        total = near[pl.ds(leaf * p, p)].astype(F32) + dot(bs_t[leaf], loc[place(0, leaf)])
        if leaf == 0:
            total = total + dot(edge_near[0], below[pl.ds(0, p)])
        if leaf == n - 1:
            total = total + dot(edge_near[1], above[pl.ds(0, p)])
        stage[pl.ds(leaf * p, p)] = total.astype(BF)
        if (leaf + 1) % per == 0:
            rows = pl.ds((leaf + 1 - per) * p, per * p)
            copy = pltpu.make_async_copy(stage.at[rows], out.at[rows], sems.at[leaf // per])
            copy.start()
            writes.append(copy)
    for copy in writes:
        copy.wait()


def shifted(array, by):
    peers = lax.axis_size("slab")
    pairs = [(i, i + by) for i in range(peers) if 0 <= i + by < peers]
    return lax.ppermute(array, "slab", pairs)


def body(charges, near_blocks, near_pattern, leaf_basis, transfers, couplings, interactions):
    leaves, panels, rank, rhs = near_blocks.shape[0], near_blocks.shape[2], leaf_basis.shape[1], charges.shape[1]
    plan = Plan(leaves, panels, rank, rhs)
    hbm = pl.BlockSpec(memory_space=pltpu.HBM)
    vmem = pl.BlockSpec(memory_space=pltpu.VMEM)
    smem = pl.BlockSpec(memory_space=pltpu.SMEM)
    chunks = 8

    padded_x, poles, up, down, top, pair_top, bs, ts = pl.pallas_call(
        lambda *refs: upward_kernel(plan, chunks, *refs),
        in_specs=[hbm, hbm, hbm],
        out_specs=[vmem] * 8,
        out_shape=[
            resident(((leaves + 2) * panels, rhs), BF),
            resident((plan.padded_boxes * rank, rhs), BF),
            resident((plan.msg_rows, rhs), BF),
            resident((plan.msg_rows, rhs), BF),
            resident((rank, rhs), BF),
            resident((2 * rank, rhs), BF),
            resident(leaf_basis.shape, BF),
            resident(transfers.shape, BF),
        ],
        scratch_shapes=[pltpu.SemaphoreType.DMA((chunks + 2,))],
        compiler_params=pltpu.CompilerParams(vmem_limit_bytes=6 * MIB),
        name="upward",
    )(stay(charges), stay(leaf_basis), stay(transfers))

    below, above = shifted(up, 1), shifted(down, -1)

    local, masked, bs_t, ts_t, up2, down2, top = pl.pallas_call(
        lambda *refs: couple_kernel(plan, *refs),
        in_specs=[smem, vmem, vmem, vmem, vmem, vmem, hbm],
        out_specs=[vmem] * 7,
        out_shape=[
            resident((plan.inner_boxes * rank, rhs), F32),
            resident(couplings.shape, BF),
            resident((leaves, panels, rank), BF),
            resident((transfers.shape[0], panels, rank), BF),
            resident((2 * rank, rhs), BF),
            resident((2 * rank, rhs), BF),
            resident((rank, rhs), BF),
        ],
        scratch_shapes=[pltpu.SemaphoreType.DMA((2,))],
        compiler_params=pltpu.CompilerParams(vmem_limit_bytes=8 * MIB),
        cost_estimate=pl.CostEstimate(flops=6_000_000_000, bytes_accessed=8 * MIB, transcendentals=0),
        name="couple",
    )(interactions.T, keep(poles), keep(bs), keep(ts), keep(top), keep(pair_top), stay(couplings))

    below2, above2 = shifted(up2, 2), shifted(down2, -2)
    below3, above3 = shifted(top, 3), shifted(top, -3)

    near, edge_near = pl.pallas_call(
        lambda *refs: near_kernel(plan, 4, *refs),
        in_specs=[smem, vmem, hbm],
        out_specs=[vmem] * 2,
        out_shape=[
            resident((leaves * panels, rhs), BF),
            resident((2, panels, panels), BF),
        ],
        scratch_shapes=[pltpu.VMEM(near_blocks.shape, BF), pltpu.SemaphoreType.DMA((4,))],
        compiler_params=pltpu.CompilerParams(vmem_limit_bytes=10 * MIB),
        cost_estimate=pl.CostEstimate(flops=6_000_000_000, bytes_accessed=8 * MIB, transcendentals=0),
        name="near",
    )(near_pattern.T, keep(padded_x), stay(near_blocks))

    return pl.pallas_call(
        lambda *refs: final_kernel(plan, *refs),
        in_specs=[vmem] * 12,
        out_specs=hbm,
        out_shape=jax.ShapeDtypeStruct((leaves * panels, rhs), BF),
        scratch_shapes=[
            pltpu.VMEM((couplings.shape[0] * rank, rhs), BF),
            pltpu.VMEM((leaves * panels, rhs), BF),
            pltpu.SemaphoreType.DMA((leaves // 4,)),
        ],
        compiler_params=pltpu.CompilerParams(vmem_limit_bytes=14 * MIB),
        name="final",
    )(
        keep(near), keep(local), keep(masked), keep(edge_near), keep(bs_t), keep(ts_t),
        keep(below), keep(above), keep(below2), keep(above2), keep(below3), keep(above3),
    )


def solution(mesh):
    spec = ("groups", "slab")
    in_specs = (
        P(spec, None),
        P(spec, None, None, None),
        P(spec, None),
        P(spec, None, None),
        P(spec, None, None),
        P(spec, None, None),
        P(spec, None),
    )
    return jax.shard_map(body, mesh=mesh, in_specs=in_specs, out_specs=P(spec, None), check_vma=False)
```

```python
import jax
import jax.numpy as jnp
from jax import lax
from jax.experimental import pallas as pl
from jax.experimental.pallas import tpu as pltpu
from jax.sharding import PartitionSpec as P

LEVELS = 6
FULL = LEVELS - 2
BF = jnp.bfloat16
F32 = jnp.float32
MIB = 1 << 20


def resident(shape, dtype):
    return pltpu.VMEM(shape, dtype)


def keep(array):
    return pltpu.with_memory_space_constraint(array, pltpu.VMEM)


def stay(array):
    return pltpu.with_memory_space_constraint(array, pltpu.HBM)


def dot(a, b):
    return lax.dot_general(a, b, (((1,), (0,)), ((), ())), preferred_element_type=F32)


class Plan:
    def __init__(self, leaves, panels, rank, rhs):
        self.leaves, self.panels, self.rank, self.rhs = leaves, panels, rank, rhs
        self.count = [leaves >> level for level in range(LEVELS)]
        self.first = [sum(self.count[:level]) for level in range(LEVELS)]
        self.trans = [0] + [sum(self.count[1:level]) for level in range(1, LEVELS)]
        self.padded = [sum(c + 6 for c in self.count[:level]) for level in range(FULL)]
        self.padded_boxes = sum(c + 6 for c in self.count[:FULL])
        self.inner_boxes = sum(self.count[:FULL])
        self.msg_pole = [panels + 2 * rank * level for level in range(FULL)]
        self.msg_top = panels + 2 * rank * FULL
        self.msg_small = self.msg_top + rank
        self.msg_last = self.msg_small + rank
        self.part_rows = rank * panels // rhs
        self.msg_rows = self.msg_last + self.part_rows


def upward_kernel(plan, chunks, charges, basis, transfers, padded_x, poles, up, down, up2, down2, top, bs, ts, pair4, sems):
    p, r = plan.panels, plan.rank
    per = plan.leaves // chunks
    copies = []
    for c in range(chunks):
        rows = per * p
        copies.append(
            pltpu.make_async_copy(
                charges.at[pl.ds(c * rows, rows)], padded_x.at[pl.ds(p + c * rows, rows)], sems.at[c]
            )
        )
    basis_copy = pltpu.make_async_copy(basis, bs, sems.at[chunks])
    trans_copy = pltpu.make_async_copy(transfers, ts, sems.at[chunks + 1])
    basis_copy.start()
    copies[0].start()
    trans_copy.start()
    for copy in copies[1:]:
        copy.start()
    padded_x[pl.ds(0, p)] = jnp.zeros((p, plan.rhs), BF)
    padded_x[pl.ds(p * (plan.leaves + 1), p)] = jnp.zeros((p, plan.rhs), BF)
    for level in range(FULL):
        start = plan.padded[level] * r
        poles[pl.ds(start, 3 * r)] = jnp.zeros((3 * r, plan.rhs), BF)
        poles[pl.ds(start + (plan.count[level] + 3) * r, 3 * r)] = jnp.zeros((3 * r, plan.rhs), BF)
    basis_copy.wait()

    def keep(level, box, value):
        n = plan.count[level]
        if level < FULL:
            poles[pl.ds((plan.padded[level] + 3 + box) * r, r)] = value
            if n - 3 <= box <= n - 2:
                up[pl.ds(plan.msg_pole[level] + (box - n + 3) * r, r)] = value
            if 1 <= box <= 2:
                down[pl.ds(plan.msg_pole[level] + (box - 1) * r, r)] = value
        elif level == FULL:
            (up if box == 0 else down)[pl.ds(plan.msg_top, r)] = value
            (down2 if box == 0 else up2)[pl.ds(0, r)] = value
            pair4[pl.ds(box * r, r)] = value
        else:
            for message in (up2, down2):
                message[pl.ds(r, r)] = value
            top[...] = value

    def climb(level, box):
        if level <= FULL:
            pair = poles[pl.ds((plan.padded[level - 1] + 3 + 2 * box) * r, 2 * r)]
        else:
            pair = pair4[...]
        keep(level, box, dot(ts[plan.trans[level] + box], pair).astype(BF))

    done = [0] * LEVELS

    def climb_ready():
        ready = list(done)
        for level in range(1, LEVELS):
            while 2 * done[level] + 2 <= ready[level - 1]:
                climb(level, done[level])
                done[level] += 1

    for c in range(chunks):
        copies[c].wait()
        if c == 0:
            trans_copy.wait()
        climb_ready()
        for leaf in range(c * per, (c + 1) * per):
            x = padded_x[pl.ds(p * (leaf + 1), p)]
            keep(0, leaf, dot(bs[leaf], x).astype(BF))
        done[0] = (c + 1) * per
    while done[LEVELS - 1] < plan.count[LEVELS - 1]:
        climb_ready()
    for message, leaf, last in ((up, plan.leaves - 1, True), (down, 0, False)):
        message[pl.ds(0, p)] = padded_x[pl.ds(p * (leaf + 1), p)]
        message[pl.ds(plan.msg_small, r), pl.ds(0, p)] = bs[leaf]
        for level in range(1, FULL):
            box = plan.count[level] - 1 if last else 0
            message[pl.ds(plan.msg_small, r), pl.ds(level * p, p)] = ts[plan.trans[level] + box]
        matrix = plan.trans[FULL] + (plan.count[FULL] - 1 if last else 0)
        rows = plan.part_rows
        for part in range(plan.rhs // p):
            message[pl.ds(plan.msg_last, rows), pl.ds(part * p, p)] = ts[matrix, pl.ds(part * rows, rows)]


def couple_kernel(
    plan, flags, poles, bs, ts, top, couplings,
    local, masked, bs_t, ts_t, top_out,
):
    p, r = plan.panels, plan.rank
    top_out[...] = top[...]
    for box in range(ts.shape[0]):
        ts_t[box] = ts[box].T
    for leaf in range(bs.shape[0]):
        bs_t[leaf] = bs[leaf].T
    lane = lax.broadcasted_iota(jnp.int32, (r, 4 * r), 1)

    def mask(box):
        low = jnp.where(lane < r, flags[0, box], flags[1, box])
        high = jnp.where(lane < 3 * r, flags[2, box], flags[3, box])
        chosen = jnp.where(lane < 2 * r, low, high)
        value = couplings[box] * chosen.astype(F32).astype(BF)
        masked[box] = value
        return value

    for level in range(FULL):
        for box in range(plan.count[level]):
            row = (plan.padded[level] + box) * r
            stack = jnp.concatenate([poles[pl.ds(row, 2 * r)], poles[pl.ds(row + 5 * r, 2 * r)]], axis=0)
            index = plan.first[level] + box
            local[pl.ds(index * r, r)] = dot(mask(index), stack)
    for box in range(plan.inner_boxes, sum(plan.count)):
        mask(box)


def near_kernel(plan, pattern, padded_x, near_blocks, near, edge_near):
    p = plan.panels

    def side(leaf, slot):
        block = near_blocks[leaf, slot]
        return jnp.where(pattern[slot, leaf] != 0, block, jnp.zeros_like(block))

    zero = jnp.zeros((p, p), BF)
    for leaf in range(0, plan.leaves, 2):
        upper = jnp.concatenate([side(leaf, 0), near_blocks[leaf, 1], side(leaf, 2), zero], axis=1)
        lower = jnp.concatenate([zero, side(leaf + 1, 0), near_blocks[leaf + 1, 1], side(leaf + 1, 2)], axis=1)
        both = jnp.concatenate([upper, lower], axis=0)
        near[pl.ds(leaf * p, 2 * p)] = dot(both, padded_x[pl.ds(leaf * p, 4 * p)]).astype(BF)
    edge_near[0] = side(0, 0)
    edge_near[1] = side(plan.leaves - 1, 2)


def final_kernel(
    plan, near, local, masked, edge_near, bs_t, ts_t, below, above, below2, above2, below3, above3,
    out, loc, stage, sems,
):
    p, r, n = plan.panels, plan.rank, plan.leaves
    small = pl.ds(plan.msg_small, r)
    messages = (below, above)

    sent = [[message[pl.ds(plan.msg_pole[level], 2 * r)] for level in range(FULL)] for message in messages]
    rim = [[dot(message[small, pl.ds(0, p)], message[pl.ds(0, p)]).astype(BF)] for message in messages]
    for level in range(1, FULL + 1):
        for k, message in enumerate(messages):
            if level < FULL:
                matrix = message[small, pl.ds(level * p, p)]
            else:
                rows = pl.ds(plan.msg_last, plan.part_rows)
                matrix = jnp.concatenate([message[rows, pl.ds(part * p, p)] for part in range(plan.rhs // p)], axis=0)
            children = [sent[k][level - 1][r:], rim[k][-1]] if k == 0 else [rim[k][-1], sent[k][level - 1][:r]]
            rim[k].append(dot(matrix, jnp.concatenate(children, axis=0)).astype(BF))

    def place(level, box):
        return pl.ds((plan.first[level] + box) * r, r)

    stack = jnp.concatenate([below3[...], below2[pl.ds(r, r)], above2[pl.ds(r, r)], above3[...]], axis=0)
    summit = dot(masked[plan.first[LEVELS - 1]], stack).astype(BF)
    pushed = dot(ts_t[plan.trans[LEVELS - 1]], summit)
    low, high = below[pl.ds(plan.msg_top, r)], above[pl.ds(plan.msg_top, r)]
    stacks = ([below2[pl.ds(0, r)], low, rim[1][FULL], high], [low, rim[0][FULL], high, above2[pl.ds(0, r)]])
    for k, stack in enumerate(stacks):
        gained = dot(masked[plan.first[FULL] + k], jnp.concatenate(stack, axis=0))
        loc[place(FULL, k)] = (gained + pushed[k * r : (k + 1) * r]).astype(BF)

    def rim_gain(level, box):
        first, m = plan.first[level], plan.count[level]
        low = [sent[0][level][:r], sent[0][level][r:], rim[0][level]]
        high = [rim[1][level], sent[1][level][:r], sent[1][level][r:]]
        gain = None
        if box < 3:
            used = low[box : box + 2]
            gain = dot(masked[first + box, :, pl.ds(0, len(used) * r)], jnp.concatenate(used, axis=0))
        if box >= m - 3:
            from_end = box - (m - 3)
            used = high[max(from_end - 1, 0) : from_end + 1]
            start = (4 - len(used)) * r if from_end == 0 else 2 * r
            value = dot(masked[first + box, :, pl.ds(start, len(used) * r)], jnp.concatenate(used, axis=0))
            gain = value if gain is None else gain + value
        return gain

    for level in range(FULL, 0, -1):
        for box in range(plan.count[level]):
            push = dot(ts_t[plan.trans[level] + box], loc[place(level, box)])
            for k in range(2):
                child = 2 * box + k
                value = local[place(level - 1, child)] + push[k * r : (k + 1) * r]
                gain = rim_gain(level - 1, child)
                loc[place(level - 1, child)] = (value if gain is None else value + gain).astype(BF)

    writes = []
    per = n // sems.shape[0]
    for leaf in range(n):
        total = near[pl.ds(leaf * p, p)].astype(F32) + dot(bs_t[leaf], loc[place(0, leaf)])
        if leaf == 0:
            total = total + dot(edge_near[0], below[pl.ds(0, p)])
        if leaf == n - 1:
            total = total + dot(edge_near[1], above[pl.ds(0, p)])
        stage[pl.ds(leaf * p, p)] = total.astype(BF)
        if (leaf + 1) % per == 0:
            rows = pl.ds((leaf + 1 - per) * p, per * p)
            copy = pltpu.make_async_copy(stage.at[rows], out.at[rows], sems.at[leaf // per])
            copy.start()
            writes.append(copy)
    for copy in writes:
        copy.wait()


def shifted(array, by):
    peers = lax.axis_size("slab")
    pairs = [(i, i + by) for i in range(peers) if 0 <= i + by < peers]
    return lax.ppermute(array, "slab", pairs)


def body(charges, near_blocks, near_pattern, leaf_basis, transfers, couplings, interactions):
    leaves, panels, rank, rhs = near_blocks.shape[0], near_blocks.shape[2], leaf_basis.shape[1], charges.shape[1]
    plan = Plan(leaves, panels, rank, rhs)
    hbm = pl.BlockSpec(memory_space=pltpu.HBM)
    vmem = pl.BlockSpec(memory_space=pltpu.VMEM)
    smem = pl.BlockSpec(memory_space=pltpu.SMEM)
    chunks = 8

    padded_x, poles, up, down, up2, down2, top, bs, ts = pl.pallas_call(
        lambda *refs: upward_kernel(plan, chunks, *refs),
        in_specs=[hbm, hbm, hbm],
        out_specs=[vmem] * 9,
        out_shape=[
            resident(((leaves + 2) * panels, rhs), BF),
            resident((plan.padded_boxes * rank, rhs), BF),
            resident((plan.msg_rows, rhs), BF),
            resident((plan.msg_rows, rhs), BF),
            resident((2 * rank, rhs), BF),
            resident((2 * rank, rhs), BF),
            resident((rank, rhs), BF),
            resident(leaf_basis.shape, BF),
            resident(transfers.shape, BF),
        ],
        scratch_shapes=[pltpu.VMEM((2 * rank, rhs), BF), pltpu.SemaphoreType.DMA((chunks + 2,))],
        compiler_params=pltpu.CompilerParams(vmem_limit_bytes=6 * MIB),
        name="upward",
    )(stay(charges), stay(leaf_basis), stay(transfers))

    below, above = shifted(up, 1), shifted(down, -1)
    below2, above2 = shifted(up2, 2), shifted(down2, -2)

    local, masked, bs_t, ts_t, top = pl.pallas_call(
        lambda *refs: couple_kernel(plan, *refs),
        in_specs=[smem, vmem, vmem, vmem, vmem, vmem],
        out_specs=[vmem] * 5,
        out_shape=[
            resident((plan.inner_boxes * rank, rhs), F32),
            resident(couplings.shape, BF),
            resident((leaves, panels, rank), BF),
            resident((transfers.shape[0], panels, rank), BF),
            resident((rank, rhs), BF),
        ],
        compiler_params=pltpu.CompilerParams(vmem_limit_bytes=8 * MIB),
        cost_estimate=pl.CostEstimate(flops=6_000_000_000, bytes_accessed=8 * MIB, transcendentals=0),
        name="couple",
    )(interactions.T, keep(poles), keep(bs), keep(ts), keep(top), keep(couplings))

    below3, above3 = shifted(top, 3), shifted(top, -3)

    near, edge_near = pl.pallas_call(
        lambda *refs: near_kernel(plan, *refs),
        in_specs=[smem, vmem, vmem],
        out_specs=[vmem] * 2,
        out_shape=[
            resident((leaves * panels, rhs), BF),
            resident((2, panels, panels), BF),
        ],
        compiler_params=pltpu.CompilerParams(vmem_limit_bytes=8 * MIB),
        cost_estimate=pl.CostEstimate(flops=6_000_000_000, bytes_accessed=8 * MIB, transcendentals=0),
        name="near",
    )(near_pattern.T, keep(padded_x), keep(near_blocks))

    return pl.pallas_call(
        lambda *refs: final_kernel(plan, *refs),
        in_specs=[vmem] * 12,
        out_specs=hbm,
        out_shape=jax.ShapeDtypeStruct((leaves * panels, rhs), BF),
        scratch_shapes=[
            pltpu.VMEM((couplings.shape[0] * rank, rhs), BF),
            pltpu.VMEM((leaves * panels, rhs), BF),
            pltpu.SemaphoreType.DMA((leaves // 4,)),
        ],
        compiler_params=pltpu.CompilerParams(vmem_limit_bytes=14 * MIB),
        name="final",
    )(
        keep(near), keep(local), keep(masked), keep(edge_near), keep(bs_t), keep(ts_t),
        keep(below), keep(above), keep(below2), keep(above2), keep(below3), keep(above3),
    )


def solution(mesh):
    spec = ("groups", "slab")
    in_specs = (
        P(spec, None),
        P(spec, None, None, None),
        P(spec, None),
        P(spec, None, None),
        P(spec, None, None),
        P(spec, None, None),
        P(spec, None),
    )
    return jax.shard_map(body, mesh=mesh, in_specs=in_specs, out_specs=P(spec, None), check_vma=False)
```

```python
import jax
import jax.numpy as jnp
from jax import lax
from jax.experimental import pallas as pl
from jax.experimental.pallas import tpu as pltpu
from jax.sharding import PartitionSpec as P

LEVELS = 6
FULL = LEVELS - 2
BF = jnp.bfloat16
F32 = jnp.float32
MIB = 1 << 20


def resident(shape, dtype):
    return pltpu.VMEM(shape, dtype)


def keep(array):
    return pltpu.with_memory_space_constraint(array, pltpu.VMEM)


def stay(array):
    return pltpu.with_memory_space_constraint(array, pltpu.HBM)


def dot(a, b):
    return lax.dot_general(a, b, (((1,), (0,)), ((), ())), preferred_element_type=F32)


class Plan:
    def __init__(self, leaves, panels, rank, rhs):
        self.leaves, self.panels, self.rank, self.rhs = leaves, panels, rank, rhs
        self.count = [leaves >> level for level in range(LEVELS)]
        self.first = [sum(self.count[:level]) for level in range(LEVELS)]
        self.trans = [0] + [sum(self.count[1:level]) for level in range(1, LEVELS)]
        self.padded = [sum(c + 6 for c in self.count[:level]) for level in range(FULL)]
        self.padded_boxes = sum(c + 6 for c in self.count[:FULL])
        self.inner_boxes = sum(self.count[:FULL])
        self.msg_pole = [panels + 2 * rank * level for level in range(FULL)]
        self.msg_top = panels + 2 * rank * FULL
        self.msg_small = self.msg_top + rank
        self.msg_last = self.msg_small + rank
        self.part_rows = rank * panels // rhs
        self.msg_rows = self.msg_last + self.part_rows


def upward_kernel(plan, chunks, charges, basis, transfers, padded_x, poles, up, down, up2, down2, top, bs, ts, pair4, sems):
    p, r = plan.panels, plan.rank
    per = plan.leaves // chunks
    copies = []
    for c in range(chunks):
        rows = per * p
        copies.append(
            pltpu.make_async_copy(
                charges.at[pl.ds(c * rows, rows)], padded_x.at[pl.ds(p + c * rows, rows)], sems.at[c]
            )
        )
    basis_copy = pltpu.make_async_copy(basis, bs, sems.at[chunks])
    trans_copy = pltpu.make_async_copy(transfers, ts, sems.at[chunks + 1])
    basis_copy.start()
    copies[0].start()
    trans_copy.start()
    for copy in copies[1:]:
        copy.start()
    padded_x[pl.ds(0, p)] = jnp.zeros((p, plan.rhs), BF)
    padded_x[pl.ds(p * (plan.leaves + 1), p)] = jnp.zeros((p, plan.rhs), BF)
    for level in range(FULL):
        start = plan.padded[level] * r
        poles[pl.ds(start, 3 * r)] = jnp.zeros((3 * r, plan.rhs), BF)
        poles[pl.ds(start + (plan.count[level] + 3) * r, 3 * r)] = jnp.zeros((3 * r, plan.rhs), BF)
    basis_copy.wait()

    def keep(level, box, value):
        n = plan.count[level]
        if level < FULL:
            poles[pl.ds((plan.padded[level] + 3 + box) * r, r)] = value
            if n - 3 <= box <= n - 2:
                up[pl.ds(plan.msg_pole[level] + (box - n + 3) * r, r)] = value
            if 1 <= box <= 2:
                down[pl.ds(plan.msg_pole[level] + (box - 1) * r, r)] = value
        elif level == FULL:
            (up if box == 0 else down)[pl.ds(plan.msg_top, r)] = value
            (down2 if box == 0 else up2)[pl.ds(0, r)] = value
            pair4[pl.ds(box * r, r)] = value
        else:
            for message in (up2, down2):
                message[pl.ds(r, r)] = value
            top[...] = value

    def climb(level, box):
        if level <= FULL:
            pair = poles[pl.ds((plan.padded[level - 1] + 3 + 2 * box) * r, 2 * r)]
        else:
            pair = pair4[...]
        keep(level, box, dot(ts[plan.trans[level] + box], pair).astype(BF))

    done = [0] * LEVELS

    def climb_ready():
        ready = list(done)
        for level in range(1, LEVELS):
            while 2 * done[level] + 2 <= ready[level - 1]:
                climb(level, done[level])
                done[level] += 1

    for c in range(chunks):
        copies[c].wait()
        if c == 0:
            trans_copy.wait()
        climb_ready()
        for leaf in range(c * per, (c + 1) * per):
            x = padded_x[pl.ds(p * (leaf + 1), p)]
            keep(0, leaf, dot(bs[leaf], x).astype(BF))
        done[0] = (c + 1) * per
    while done[LEVELS - 1] < plan.count[LEVELS - 1]:
        climb_ready()
    for message, leaf, last in ((up, plan.leaves - 1, True), (down, 0, False)):
        message[pl.ds(0, p)] = padded_x[pl.ds(p * (leaf + 1), p)]
        message[pl.ds(plan.msg_small, r), pl.ds(0, p)] = bs[leaf]
        for level in range(1, FULL):
            box = plan.count[level] - 1 if last else 0
            message[pl.ds(plan.msg_small, r), pl.ds(level * p, p)] = ts[plan.trans[level] + box]
        matrix = plan.trans[FULL] + (plan.count[FULL] - 1 if last else 0)
        rows = plan.part_rows
        for part in range(plan.rhs // p):
            message[pl.ds(plan.msg_last, rows), pl.ds(part * p, p)] = ts[matrix, pl.ds(part * rows, rows)]


def couple_kernel(
    plan, flags, poles, bs, ts, couplings,
    local, masked, bs_t, ts_t,
):
    p, r = plan.panels, plan.rank
    for box in range(ts.shape[0]):
        ts_t[box] = ts[box].T
    for leaf in range(bs.shape[0]):
        bs_t[leaf] = bs[leaf].T
    lane = lax.broadcasted_iota(jnp.int32, (r, 4 * r), 1)

    def mask(box):
        low = jnp.where(lane < r, flags[0, box], flags[1, box])
        high = jnp.where(lane < 3 * r, flags[2, box], flags[3, box])
        chosen = jnp.where(lane < 2 * r, low, high)
        value = couplings[box] * chosen.astype(F32).astype(BF)
        masked[box] = value
        return value

    for level in range(FULL):
        for box in range(plan.count[level]):
            row = (plan.padded[level] + box) * r
            stack = jnp.concatenate([poles[pl.ds(row, 2 * r)], poles[pl.ds(row + 5 * r, 2 * r)]], axis=0)
            index = plan.first[level] + box
            local[pl.ds(index * r, r)] = dot(mask(index), stack)
    for box in range(plan.inner_boxes, sum(plan.count)):
        mask(box)


def near_kernel(plan, pattern, padded_x, near_blocks, near, edge_near):
    p = plan.panels

    def side(leaf, slot):
        block = near_blocks[leaf, slot]
        return jnp.where(pattern[slot, leaf] != 0, block, jnp.zeros_like(block))

    zero = jnp.zeros((p, p), BF)
    for leaf in range(0, plan.leaves, 2):
        upper = jnp.concatenate([side(leaf, 0), near_blocks[leaf, 1], side(leaf, 2), zero], axis=1)
        lower = jnp.concatenate([zero, side(leaf + 1, 0), near_blocks[leaf + 1, 1], side(leaf + 1, 2)], axis=1)
        both = jnp.concatenate([upper, lower], axis=0)
        near[pl.ds(leaf * p, 2 * p)] = dot(both, padded_x[pl.ds(leaf * p, 4 * p)]).astype(BF)
    edge_near[0] = side(0, 0)
    edge_near[1] = side(plan.leaves - 1, 2)


def final_kernel(
    plan, near, local, masked, edge_near, bs_t, ts_t, below3, above3, below2, above2, below, above,
    out, loc, stage, sems,
):
    p, r, n = plan.panels, plan.rank, plan.leaves
    small = pl.ds(plan.msg_small, r)
    messages = (below, above)

    sent = [[message[pl.ds(plan.msg_pole[level], 2 * r)] for level in range(FULL)] for message in messages]
    rim = [[dot(message[small, pl.ds(0, p)], message[pl.ds(0, p)]).astype(BF)] for message in messages]
    for level in range(1, FULL + 1):
        for k, message in enumerate(messages):
            if level < FULL:
                matrix = message[small, pl.ds(level * p, p)]
            else:
                rows = pl.ds(plan.msg_last, plan.part_rows)
                matrix = jnp.concatenate([message[rows, pl.ds(part * p, p)] for part in range(plan.rhs // p)], axis=0)
            children = [sent[k][level - 1][r:], rim[k][-1]] if k == 0 else [rim[k][-1], sent[k][level - 1][:r]]
            rim[k].append(dot(matrix, jnp.concatenate(children, axis=0)).astype(BF))

    def place(level, box):
        return pl.ds((plan.first[level] + box) * r, r)

    stack = jnp.concatenate([below3[...], below2[pl.ds(r, r)], above2[pl.ds(r, r)], above3[...]], axis=0)
    summit = dot(masked[plan.first[LEVELS - 1]], stack).astype(BF)
    pushed = dot(ts_t[plan.trans[LEVELS - 1]], summit)
    low, high = below[pl.ds(plan.msg_top, r)], above[pl.ds(plan.msg_top, r)]
    stacks = ([below2[pl.ds(0, r)], low, rim[1][FULL], high], [low, rim[0][FULL], high, above2[pl.ds(0, r)]])
    for k, stack in enumerate(stacks):
        gained = dot(masked[plan.first[FULL] + k], jnp.concatenate(stack, axis=0))
        loc[place(FULL, k)] = (gained + pushed[k * r : (k + 1) * r]).astype(BF)

    def rim_gain(level, box):
        first, m = plan.first[level], plan.count[level]
        low = [sent[0][level][:r], sent[0][level][r:], rim[0][level]]
        high = [rim[1][level], sent[1][level][:r], sent[1][level][r:]]
        gain = None
        if box < 3:
            used = low[box : box + 2]
            gain = dot(masked[first + box, :, pl.ds(0, len(used) * r)], jnp.concatenate(used, axis=0))
        if box >= m - 3:
            from_end = box - (m - 3)
            used = high[max(from_end - 1, 0) : from_end + 1]
            start = (4 - len(used)) * r if from_end == 0 else 2 * r
            value = dot(masked[first + box, :, pl.ds(start, len(used) * r)], jnp.concatenate(used, axis=0))
            gain = value if gain is None else gain + value
        return gain

    for level in range(FULL, 0, -1):
        for box in range(plan.count[level]):
            push = dot(ts_t[plan.trans[level] + box], loc[place(level, box)])
            for k in range(2):
                child = 2 * box + k
                value = local[place(level - 1, child)] + push[k * r : (k + 1) * r]
                gain = rim_gain(level - 1, child)
                loc[place(level - 1, child)] = (value if gain is None else value + gain).astype(BF)

    writes = []
    per = n // sems.shape[0]
    for leaf in range(n):
        total = near[pl.ds(leaf * p, p)].astype(F32) + dot(bs_t[leaf], loc[place(0, leaf)])
        if leaf == 0:
            total = total + dot(edge_near[0], below[pl.ds(0, p)])
        if leaf == n - 1:
            total = total + dot(edge_near[1], above[pl.ds(0, p)])
        stage[pl.ds(leaf * p, p)] = total.astype(BF)
        if (leaf + 1) % per == 0:
            rows = pl.ds((leaf + 1 - per) * p, per * p)
            copy = pltpu.make_async_copy(stage.at[rows], out.at[rows], sems.at[leaf // per])
            copy.start()
            writes.append(copy)
    for copy in writes:
        copy.wait()


def shifted(array, by):
    peers = lax.axis_size("slab")
    pairs = [(i, i + by) for i in range(peers) if 0 <= i + by < peers]
    return lax.ppermute(array, "slab", pairs)


def body(charges, near_blocks, near_pattern, leaf_basis, transfers, couplings, interactions):
    leaves, panels, rank, rhs = near_blocks.shape[0], near_blocks.shape[2], leaf_basis.shape[1], charges.shape[1]
    plan = Plan(leaves, panels, rank, rhs)
    hbm = pl.BlockSpec(memory_space=pltpu.HBM)
    vmem = pl.BlockSpec(memory_space=pltpu.VMEM)
    smem = pl.BlockSpec(memory_space=pltpu.SMEM)
    chunks = 8

    padded_x, poles, up, down, up2, down2, top, bs, ts = pl.pallas_call(
        lambda *refs: upward_kernel(plan, chunks, *refs),
        in_specs=[hbm, hbm, hbm],
        out_specs=[vmem] * 9,
        out_shape=[
            resident(((leaves + 2) * panels, rhs), BF),
            resident((plan.padded_boxes * rank, rhs), BF),
            resident((plan.msg_rows, rhs), BF),
            resident((plan.msg_rows, rhs), BF),
            resident((2 * rank, rhs), BF),
            resident((2 * rank, rhs), BF),
            resident((rank, rhs), BF),
            resident(leaf_basis.shape, BF),
            resident(transfers.shape, BF),
        ],
        scratch_shapes=[pltpu.VMEM((2 * rank, rhs), BF), pltpu.SemaphoreType.DMA((chunks + 2,))],
        compiler_params=pltpu.CompilerParams(vmem_limit_bytes=6 * MIB),
        name="upward",
    )(stay(charges), stay(leaf_basis), stay(transfers))

    below, above = shifted(up, 1), shifted(down, -1)
    below2, above2 = shifted(up2, 2), shifted(down2, -2)
    below3, above3 = shifted(top, 3), shifted(top, -3)

    local, masked, bs_t, ts_t = pl.pallas_call(
        lambda *refs: couple_kernel(plan, *refs),
        in_specs=[smem, vmem, vmem, vmem, vmem],
        out_specs=[vmem] * 4,
        out_shape=[
            resident((plan.inner_boxes * rank, rhs), F32),
            resident(couplings.shape, BF),
            resident((leaves, panels, rank), BF),
            resident((transfers.shape[0], panels, rank), BF),
        ],
        compiler_params=pltpu.CompilerParams(vmem_limit_bytes=8 * MIB),
        cost_estimate=pl.CostEstimate(flops=6_000_000_000, bytes_accessed=8 * MIB, transcendentals=0),
        name="couple",
    )(interactions.T, keep(poles), keep(bs), keep(ts), keep(couplings))


    near, edge_near = pl.pallas_call(
        lambda *refs: near_kernel(plan, *refs),
        in_specs=[smem, vmem, vmem],
        out_specs=[vmem] * 2,
        out_shape=[
            resident((leaves * panels, rhs), BF),
            resident((2, panels, panels), BF),
        ],
        compiler_params=pltpu.CompilerParams(vmem_limit_bytes=8 * MIB),
        cost_estimate=pl.CostEstimate(flops=100_000_000, bytes_accessed=MIB // 4, transcendentals=0),
        name="near",
    )(near_pattern.T, keep(padded_x), keep(near_blocks))

    return pl.pallas_call(
        lambda *refs: final_kernel(plan, *refs),
        in_specs=[vmem] * 12,
        out_specs=hbm,
        out_shape=jax.ShapeDtypeStruct((leaves * panels, rhs), BF),
        scratch_shapes=[
            pltpu.VMEM((couplings.shape[0] * rank, rhs), BF),
            pltpu.VMEM((leaves * panels, rhs), BF),
            pltpu.SemaphoreType.DMA((leaves // 4,)),
        ],
        compiler_params=pltpu.CompilerParams(vmem_limit_bytes=14 * MIB),
        name="final",
    )(
        keep(near), keep(local), keep(masked), keep(edge_near), keep(bs_t), keep(ts_t),
        keep(below3), keep(above3), keep(below2), keep(above2), keep(below), keep(above),
    )


def solution(mesh):
    spec = ("groups", "slab")
    in_specs = (
        P(spec, None),
        P(spec, None, None, None),
        P(spec, None),
        P(spec, None, None),
        P(spec, None, None),
        P(spec, None, None),
        P(spec, None),
    )
    return jax.shard_map(body, mesh=mesh, in_specs=in_specs, out_specs=P(spec, None), check_vma=False)
```

```python
import jax
import jax.numpy as jnp
from jax import lax
from jax.experimental import pallas as pl
from jax.experimental.pallas import tpu as pltpu
from jax.sharding import PartitionSpec as P

LEVELS = 6
FULL = LEVELS - 2
BF = jnp.bfloat16
F32 = jnp.float32
MIB = 1 << 20


def resident(shape, dtype):
    return pltpu.VMEM(shape, dtype)


def keep(array):
    return pltpu.with_memory_space_constraint(array, pltpu.VMEM)


def stay(array):
    return pltpu.with_memory_space_constraint(array, pltpu.HBM)


def dot(a, b):
    return lax.dot_general(a, b, (((1,), (0,)), ((), ())), preferred_element_type=F32)


class Plan:
    def __init__(self, leaves, panels, rank, rhs):
        self.leaves, self.panels, self.rank, self.rhs = leaves, panels, rank, rhs
        self.count = [leaves >> level for level in range(LEVELS)]
        self.first = [sum(self.count[:level]) for level in range(LEVELS)]
        self.trans = [0] + [sum(self.count[1:level]) for level in range(1, LEVELS)]
        self.padded = [sum(c + 6 for c in self.count[:level]) for level in range(FULL)]
        self.padded_boxes = sum(c + 6 for c in self.count[:FULL])
        self.inner_boxes = sum(self.count[:FULL])
        self.msg_pole = [panels + 2 * rank * level for level in range(FULL)]
        self.msg_top = panels + 2 * rank * FULL
        self.msg_small = self.msg_top + rank
        self.msg_last = self.msg_small + rank
        self.part_rows = rank * panels // rhs
        self.msg_rows = self.msg_last + self.part_rows


def upward_kernel(plan, chunks, charges, basis, transfers, padded_x, poles, up, down, pair4, bs, ts, sems):
    p, r = plan.panels, plan.rank
    per = plan.leaves // chunks
    copies = []
    for c in range(chunks):
        rows = per * p
        copies.append(
            pltpu.make_async_copy(
                charges.at[pl.ds(c * rows, rows)], padded_x.at[pl.ds(p + c * rows, rows)], sems.at[c]
            )
        )
    basis_copy = pltpu.make_async_copy(basis, bs, sems.at[chunks])
    trans_copy = pltpu.make_async_copy(transfers, ts, sems.at[chunks + 1])
    basis_copy.start()
    copies[0].start()
    trans_copy.start()
    for copy in copies[1:]:
        copy.start()
    padded_x[pl.ds(0, p)] = jnp.zeros((p, plan.rhs), BF)
    padded_x[pl.ds(p * (plan.leaves + 1), p)] = jnp.zeros((p, plan.rhs), BF)
    for level in range(FULL):
        start = plan.padded[level] * r
        poles[pl.ds(start, 3 * r)] = jnp.zeros((3 * r, plan.rhs), BF)
        poles[pl.ds(start + (plan.count[level] + 3) * r, 3 * r)] = jnp.zeros((3 * r, plan.rhs), BF)
    basis_copy.wait()

    def keep(level, box, value):
        n = plan.count[level]
        if level < FULL:
            poles[pl.ds((plan.padded[level] + 3 + box) * r, r)] = value
            if n - 3 <= box <= n - 2:
                up[pl.ds(plan.msg_pole[level] + (box - n + 3) * r, r)] = value
            if 1 <= box <= 2:
                down[pl.ds(plan.msg_pole[level] + (box - 1) * r, r)] = value
        elif level == FULL:
            (up if box == 0 else down)[pl.ds(plan.msg_top, r)] = value
            pair4[pl.ds(box * r, r)] = value

    def climb(level, box):
        pair = poles[pl.ds((plan.padded[level - 1] + 3 + 2 * box) * r, 2 * r)]
        keep(level, box, dot(ts[plan.trans[level] + box], pair).astype(BF))

    done = [0] * (FULL + 1)

    def climb_ready():
        ready = list(done)
        for level in range(1, FULL + 1):
            while 2 * done[level] + 2 <= ready[level - 1]:
                climb(level, done[level])
                done[level] += 1

    for c in range(chunks):
        copies[c].wait()
        if c == 1:
            trans_copy.wait()
        climb_ready()
        for leaf in range(c * per, (c + 1) * per):
            x = padded_x[pl.ds(p * (leaf + 1), p)]
            keep(0, leaf, dot(bs[leaf], x).astype(BF))
        done[0] = (c + 1) * per
    while done[FULL] < plan.count[FULL]:
        climb_ready()
    for message, leaf, last in ((up, plan.leaves - 1, True), (down, 0, False)):
        message[pl.ds(0, p)] = padded_x[pl.ds(p * (leaf + 1), p)]
        message[pl.ds(plan.msg_small, r), pl.ds(0, p)] = bs[leaf]
        for level in range(1, FULL):
            box = plan.count[level] - 1 if last else 0
            message[pl.ds(plan.msg_small, r), pl.ds(level * p, p)] = ts[plan.trans[level] + box]
        matrix = plan.trans[FULL] + (plan.count[FULL] - 1 if last else 0)
        rows = plan.part_rows
        for part in range(plan.rhs // p):
            message[pl.ds(plan.msg_last, rows), pl.ds(part * p, p)] = ts[matrix, pl.ds(part * rows, rows)]


def couple_kernel(
    plan, flags, poles, bs, ts, pair4, couplings,
    local, masked, bs_t, ts_t, up2, down2, top,
):
    p, r = plan.panels, plan.rank
    summit = dot(ts[plan.trans[LEVELS - 1]], pair4[...]).astype(BF)
    up2[pl.ds(0, r)] = pair4[pl.ds(r, r)]
    down2[pl.ds(0, r)] = pair4[pl.ds(0, r)]
    for message in (up2, down2):
        message[pl.ds(r, r)] = summit
    top[...] = summit
    for box in range(ts.shape[0]):
        ts_t[box] = ts[box].T
    for leaf in range(bs.shape[0]):
        bs_t[leaf] = bs[leaf].T
    lane = lax.broadcasted_iota(jnp.int32, (r, 4 * r), 1)

    def mask(box):
        low = jnp.where(lane < r, flags[0, box], flags[1, box])
        high = jnp.where(lane < 3 * r, flags[2, box], flags[3, box])
        chosen = jnp.where(lane < 2 * r, low, high)
        value = couplings[box] * chosen.astype(F32).astype(BF)
        masked[box] = value
        return value

    for level in range(FULL):
        for box in range(plan.count[level]):
            row = (plan.padded[level] + box) * r
            stack = jnp.concatenate([poles[pl.ds(row, 2 * r)], poles[pl.ds(row + 5 * r, 2 * r)]], axis=0)
            index = plan.first[level] + box
            local[pl.ds(index * r, r)] = dot(mask(index), stack)
    for box in range(plan.inner_boxes, sum(plan.count)):
        mask(box)


def near_kernel(plan, pattern, padded_x, near_blocks, near, edge_near):
    p = plan.panels

    def side(leaf, slot):
        block = near_blocks[leaf, slot]
        return jnp.where(pattern[slot, leaf] != 0, block, jnp.zeros_like(block))

    zero = jnp.zeros((p, p), BF)
    for leaf in range(0, plan.leaves, 2):
        upper = jnp.concatenate([side(leaf, 0), near_blocks[leaf, 1], side(leaf, 2), zero], axis=1)
        lower = jnp.concatenate([zero, side(leaf + 1, 0), near_blocks[leaf + 1, 1], side(leaf + 1, 2)], axis=1)
        both = jnp.concatenate([upper, lower], axis=0)
        near[pl.ds(leaf * p, 2 * p)] = dot(both, padded_x[pl.ds(leaf * p, 4 * p)]).astype(BF)
    edge_near[0] = side(0, 0)
    edge_near[1] = side(plan.leaves - 1, 2)


def final_kernel(
    plan, near, local, masked, edge_near, bs_t, ts_t, below, above, below2, above2, below3, above3,
    out, loc, stage, sems,
):
    p, r, n = plan.panels, plan.rank, plan.leaves
    small = pl.ds(plan.msg_small, r)
    messages = (below, above)

    sent = [[message[pl.ds(plan.msg_pole[level], 2 * r)] for level in range(FULL)] for message in messages]
    rim = [[dot(message[small, pl.ds(0, p)], message[pl.ds(0, p)]).astype(BF)] for message in messages]
    for level in range(1, FULL + 1):
        for k, message in enumerate(messages):
            if level < FULL:
                matrix = message[small, pl.ds(level * p, p)]
            else:
                rows = pl.ds(plan.msg_last, plan.part_rows)
                matrix = jnp.concatenate([message[rows, pl.ds(part * p, p)] for part in range(plan.rhs // p)], axis=0)
            children = [sent[k][level - 1][r:], rim[k][-1]] if k == 0 else [rim[k][-1], sent[k][level - 1][:r]]
            rim[k].append(dot(matrix, jnp.concatenate(children, axis=0)).astype(BF))

    def place(level, box):
        return pl.ds((plan.first[level] + box) * r, r)

    stack = jnp.concatenate([below3[...], below2[pl.ds(r, r)], above2[pl.ds(r, r)], above3[...]], axis=0)
    summit = dot(masked[plan.first[LEVELS - 1]], stack).astype(BF)
    pushed = dot(ts_t[plan.trans[LEVELS - 1]], summit)
    low, high = below[pl.ds(plan.msg_top, r)], above[pl.ds(plan.msg_top, r)]
    stacks = ([below2[pl.ds(0, r)], low, rim[1][FULL], high], [low, rim[0][FULL], high, above2[pl.ds(0, r)]])
    for k, stack in enumerate(stacks):
        gained = dot(masked[plan.first[FULL] + k], jnp.concatenate(stack, axis=0))
        loc[place(FULL, k)] = (gained + pushed[k * r : (k + 1) * r]).astype(BF)

    def rim_gain(level, box):
        first, m = plan.first[level], plan.count[level]
        low = [sent[0][level][:r], sent[0][level][r:], rim[0][level]]
        high = [rim[1][level], sent[1][level][:r], sent[1][level][r:]]
        gain = None
        if box < 3:
            used = low[box : box + 2]
            gain = dot(masked[first + box, :, pl.ds(0, len(used) * r)], jnp.concatenate(used, axis=0))
        if box >= m - 3:
            from_end = box - (m - 3)
            used = high[max(from_end - 1, 0) : from_end + 1]
            start = (4 - len(used)) * r if from_end == 0 else 2 * r
            value = dot(masked[first + box, :, pl.ds(start, len(used) * r)], jnp.concatenate(used, axis=0))
            gain = value if gain is None else gain + value
        return gain

    def descend(level, box):
        push = dot(ts_t[plan.trans[level] + box], loc[place(level, box)])
        for k in range(2):
            child = 2 * box + k
            value = local[place(level - 1, child)] + push[k * r : (k + 1) * r]
            gain = rim_gain(level - 1, child)
            loc[place(level - 1, child)] = (value if gain is None else value + gain).astype(BF)

    for level in range(FULL, 1, -1):
        for box in range(plan.count[level]):
            descend(level, box)

    writes = []
    groups = sems.shape[0]
    per = n // groups

    def descend_group(group):
        for box in range(group * per // 2, (group + 1) * per // 2):
            descend(1, box)

    descend_group(0)
    for group in range(groups):
        if group + 1 < groups:
            descend_group(group + 1)
        for leaf in range(group * per, (group + 1) * per):
            total = near[pl.ds(leaf * p, p)].astype(F32) + dot(bs_t[leaf], loc[place(0, leaf)])
            if leaf == 0:
                total = total + dot(edge_near[0], below[pl.ds(0, p)])
            if leaf == n - 1:
                total = total + dot(edge_near[1], above[pl.ds(0, p)])
            stage[pl.ds(leaf * p, p)] = total.astype(BF)
        rows = pl.ds(group * per * p, per * p)
        copy = pltpu.make_async_copy(stage.at[rows], out.at[rows], sems.at[group])
        copy.start()
        writes.append(copy)
    for copy in writes:
        copy.wait()


def shifted(array, by):
    peers = lax.axis_size("slab")
    pairs = [(i, i + by) for i in range(peers) if 0 <= i + by < peers]
    return lax.ppermute(array, "slab", pairs)


def body(charges, near_blocks, near_pattern, leaf_basis, transfers, couplings, interactions):
    leaves, panels, rank, rhs = near_blocks.shape[0], near_blocks.shape[2], leaf_basis.shape[1], charges.shape[1]
    plan = Plan(leaves, panels, rank, rhs)
    hbm = pl.BlockSpec(memory_space=pltpu.HBM)
    vmem = pl.BlockSpec(memory_space=pltpu.VMEM)
    smem = pl.BlockSpec(memory_space=pltpu.SMEM)
    chunks = 8

    padded_x, poles, up, down, pair4, bs, ts = pl.pallas_call(
        lambda *refs: upward_kernel(plan, chunks, *refs),
        in_specs=[hbm, hbm, hbm],
        out_specs=[vmem] * 7,
        out_shape=[
            resident(((leaves + 2) * panels, rhs), BF),
            resident((plan.padded_boxes * rank, rhs), BF),
            resident((plan.msg_rows, rhs), BF),
            resident((plan.msg_rows, rhs), BF),
            resident((2 * rank, rhs), BF),
            resident(leaf_basis.shape, BF),
            resident(transfers.shape, BF),
        ],
        scratch_shapes=[pltpu.SemaphoreType.DMA((chunks + 2,))],
        compiler_params=pltpu.CompilerParams(vmem_limit_bytes=6 * MIB),
        name="upward",
    )(stay(charges), stay(leaf_basis), stay(transfers))

    below, above = shifted(up, 1), shifted(down, -1)

    local, masked, bs_t, ts_t, up2, down2, top = pl.pallas_call(
        lambda *refs: couple_kernel(plan, *refs),
        in_specs=[smem, vmem, vmem, vmem, vmem, vmem],
        out_specs=[vmem] * 7,
        out_shape=[
            resident((plan.inner_boxes * rank, rhs), F32),
            resident(couplings.shape, BF),
            resident((leaves, panels, rank), BF),
            resident((transfers.shape[0], panels, rank), BF),
            resident((2 * rank, rhs), BF),
            resident((2 * rank, rhs), BF),
            resident((rank, rhs), BF),
        ],
        compiler_params=pltpu.CompilerParams(vmem_limit_bytes=8 * MIB),
        cost_estimate=pl.CostEstimate(flops=6_000_000_000, bytes_accessed=8 * MIB, transcendentals=0),
        name="couple",
    )(interactions.T, keep(poles), keep(bs), keep(ts), keep(pair4), keep(couplings))

    below2, above2 = shifted(up2, 2), shifted(down2, -2)
    below3, above3 = shifted(top, 3), shifted(top, -3)

    near, edge_near = pl.pallas_call(
        lambda *refs: near_kernel(plan, *refs),
        in_specs=[smem, vmem, vmem],
        out_specs=[vmem] * 2,
        out_shape=[
            resident((leaves * panels, rhs), BF),
            resident((2, panels, panels), BF),
        ],
        compiler_params=pltpu.CompilerParams(vmem_limit_bytes=8 * MIB),
        cost_estimate=pl.CostEstimate(flops=6_000_000_000, bytes_accessed=8 * MIB, transcendentals=0),
        name="near",
    )(near_pattern.T, keep(padded_x), keep(near_blocks))

    return pl.pallas_call(
        lambda *refs: final_kernel(plan, *refs),
        in_specs=[vmem] * 12,
        out_specs=hbm,
        out_shape=jax.ShapeDtypeStruct((leaves * panels, rhs), BF),
        scratch_shapes=[
            pltpu.VMEM((couplings.shape[0] * rank, rhs), BF),
            pltpu.VMEM((leaves * panels, rhs), BF),
            pltpu.SemaphoreType.DMA((leaves // 4,)),
        ],
        compiler_params=pltpu.CompilerParams(vmem_limit_bytes=14 * MIB),
        name="final",
    )(
        keep(near), keep(local), keep(masked), keep(edge_near), keep(bs_t), keep(ts_t),
        keep(below), keep(above), keep(below2), keep(above2), keep(below3), keep(above3),
    )


def solution(mesh):
    spec = ("groups", "slab")
    in_specs = (
        P(spec, None),
        P(spec, None, None, None),
        P(spec, None),
        P(spec, None, None),
        P(spec, None, None),
        P(spec, None, None),
        P(spec, None),
    )
    return jax.shard_map(body, mesh=mesh, in_specs=in_specs, out_specs=P(spec, None), check_vma=False)
```

```python
import jax
import jax.numpy as jnp
from jax import lax
from jax.experimental import pallas as pl
from jax.experimental.pallas import tpu as pltpu
from jax.sharding import PartitionSpec as P

LEVELS = 6
FULL = LEVELS - 2
BF = jnp.bfloat16
F32 = jnp.float32
MIB = 1 << 20


def resident(shape, dtype):
    return pltpu.VMEM(shape, dtype)


def keep(array):
    return pltpu.with_memory_space_constraint(array, pltpu.VMEM)


def stay(array):
    return pltpu.with_memory_space_constraint(array, pltpu.HBM)


def dot(a, b):
    return lax.dot_general(a, b, (((1,), (0,)), ((), ())), preferred_element_type=F32)


class Plan:
    def __init__(self, leaves, panels, rank, rhs):
        self.leaves, self.panels, self.rank, self.rhs = leaves, panels, rank, rhs
        self.count = [leaves >> level for level in range(LEVELS)]
        self.first = [sum(self.count[:level]) for level in range(LEVELS)]
        self.trans = [0] + [sum(self.count[1:level]) for level in range(1, LEVELS)]
        self.padded = [sum(c + 6 for c in self.count[:level]) for level in range(FULL)]
        self.padded_boxes = sum(c + 6 for c in self.count[:FULL])
        self.inner_boxes = sum(self.count[:FULL])
        self.rim, self.rim_boxes = [], 0
        for m in self.count[:FULL]:
            boxes = sorted({0, 1, 2, m - 3, m - 2, m - 1})
            self.rim.append({box: self.rim_boxes + k for k, box in enumerate(boxes)})
            self.rim_boxes += len(boxes)
        self.msg_pole = [panels + 2 * rank * level for level in range(FULL)]
        self.msg_top = panels + 2 * rank * FULL
        self.msg_small = self.msg_top + rank
        self.msg_last = self.msg_small + rank
        self.part_rows = rank * panels // rhs
        self.msg_rows = self.msg_last + self.part_rows


def upward_kernel(plan, chunks, charges, basis, transfers, padded_x, poles, up, down, pair4, bs, ts, sems):
    p, r = plan.panels, plan.rank
    per = plan.leaves // chunks
    copies = []
    for c in range(chunks):
        rows = per * p
        copies.append(
            pltpu.make_async_copy(
                charges.at[pl.ds(c * rows, rows)], padded_x.at[pl.ds(p + c * rows, rows)], sems.at[c]
            )
        )
    basis_copy = pltpu.make_async_copy(basis, bs, sems.at[chunks])
    trans_copy = pltpu.make_async_copy(transfers, ts, sems.at[chunks + 1])
    basis_copy.start()
    copies[0].start()
    trans_copy.start()
    for copy in copies[1:]:
        copy.start()
    padded_x[pl.ds(0, p)] = jnp.zeros((p, plan.rhs), BF)
    padded_x[pl.ds(p * (plan.leaves + 1), p)] = jnp.zeros((p, plan.rhs), BF)
    for level in range(FULL):
        start = plan.padded[level] * r
        poles[pl.ds(start, 3 * r)] = jnp.zeros((3 * r, plan.rhs), BF)
        poles[pl.ds(start + (plan.count[level] + 3) * r, 3 * r)] = jnp.zeros((3 * r, plan.rhs), BF)
    basis_copy.wait()

    def keep(level, box, value):
        n = plan.count[level]
        if level < FULL:
            poles[pl.ds((plan.padded[level] + 3 + box) * r, r)] = value
            if n - 3 <= box <= n - 2:
                up[pl.ds(plan.msg_pole[level] + (box - n + 3) * r, r)] = value
            if 1 <= box <= 2:
                down[pl.ds(plan.msg_pole[level] + (box - 1) * r, r)] = value
        elif level == FULL:
            (up if box == 0 else down)[pl.ds(plan.msg_top, r)] = value
            pair4[pl.ds(box * r, r)] = value

    def climb(level, box):
        pair = poles[pl.ds((plan.padded[level - 1] + 3 + 2 * box) * r, 2 * r)]
        keep(level, box, dot(ts[plan.trans[level] + box], pair).astype(BF))

    done = [0] * (FULL + 1)

    def climb_ready():
        ready = list(done)
        for level in range(1, FULL + 1):
            while 2 * done[level] + 2 <= ready[level - 1]:
                climb(level, done[level])
                done[level] += 1

    for c in range(chunks):
        copies[c].wait()
        if c == 1:
            trans_copy.wait()
        climb_ready()
        for leaf in range(c * per, (c + 1) * per):
            x = padded_x[pl.ds(p * (leaf + 1), p)]
            keep(0, leaf, dot(bs[leaf], x).astype(BF))
        done[0] = (c + 1) * per
    while done[FULL] < plan.count[FULL]:
        climb_ready()
    for message, leaf, last in ((up, plan.leaves - 1, True), (down, 0, False)):
        message[pl.ds(0, p)] = padded_x[pl.ds(p * (leaf + 1), p)]
        message[pl.ds(plan.msg_small, r), pl.ds(0, p)] = bs[leaf]
        for level in range(1, FULL):
            box = plan.count[level] - 1 if last else 0
            message[pl.ds(plan.msg_small, r), pl.ds(level * p, p)] = ts[plan.trans[level] + box]
        matrix = plan.trans[FULL] + (plan.count[FULL] - 1 if last else 0)
        rows = plan.part_rows
        for part in range(plan.rhs // p):
            message[pl.ds(plan.msg_last, rows), pl.ds(part * p, p)] = ts[matrix, pl.ds(part * rows, rows)]


def couple_kernel(
    plan, flags, poles, bs, ts, pair4, couplings,
    local, masked, bs_t, ts_t, up2, down2, top,
):
    p, r = plan.panels, plan.rank
    summit = dot(ts[plan.trans[LEVELS - 1]], pair4[...]).astype(BF)
    up2[pl.ds(0, r)] = pair4[pl.ds(r, r)]
    down2[pl.ds(0, r)] = pair4[pl.ds(0, r)]
    for message in (up2, down2):
        message[pl.ds(r, r)] = summit
    top[...] = summit
    for box in range(ts.shape[0]):
        ts_t[box] = ts[box].T
    for leaf in range(bs.shape[0]):
        bs_t[leaf] = bs[leaf].T
    lane = lax.broadcasted_iota(jnp.int32, (r, 4 * r), 1)

    def mask(box):
        low = jnp.where(lane < r, flags[0, box], flags[1, box])
        high = jnp.where(lane < 3 * r, flags[2, box], flags[3, box])
        chosen = jnp.where(lane < 2 * r, low, high)
        value = couplings[box] * chosen.astype(F32).astype(BF)
        masked[box] = value
        return value

    for level in range(FULL):
        for box in range(plan.count[level]):
            row = (plan.padded[level] + box) * r
            stack = jnp.concatenate([poles[pl.ds(row, 2 * r)], poles[pl.ds(row + 5 * r, 2 * r)]], axis=0)
            index = plan.first[level] + box
            local[pl.ds(index * r, r)] = dot(mask(index), stack)
    for box in range(plan.inner_boxes, sum(plan.count)):
        mask(box)


def near_kernel(plan, pattern, padded_x, near_blocks, near, edge_near):
    p = plan.panels

    def side(leaf, slot):
        block = near_blocks[leaf, slot]
        return jnp.where(pattern[slot, leaf] != 0, block, jnp.zeros_like(block))

    zero = jnp.zeros((p, p), BF)
    for leaf in range(0, plan.leaves, 2):
        upper = jnp.concatenate([side(leaf, 0), near_blocks[leaf, 1], side(leaf, 2), zero], axis=1)
        lower = jnp.concatenate([zero, side(leaf + 1, 0), near_blocks[leaf + 1, 1], side(leaf + 1, 2)], axis=1)
        both = jnp.concatenate([upper, lower], axis=0)
        near[pl.ds(leaf * p, 2 * p)] = dot(both, padded_x[pl.ds(leaf * p, 4 * p)]).astype(BF)
    edge_near[0] = side(0, 0)
    edge_near[1] = side(plan.leaves - 1, 2)


def rim_kernel(plan, local, masked, below, above, below3, above3, rims, outermost, summit):
    p, r = plan.panels, plan.rank
    small = pl.ds(plan.msg_small, r)
    messages = (below, above)

    sent = [[message[pl.ds(plan.msg_pole[level], 2 * r)] for level in range(FULL)] for message in messages]
    rim = [[dot(message[small, pl.ds(0, p)], message[pl.ds(0, p)]).astype(BF)] for message in messages]
    for level in range(1, FULL + 1):
        for k, message in enumerate(messages):
            if level < FULL:
                matrix = message[small, pl.ds(level * p, p)]
            else:
                rows = pl.ds(plan.msg_last, plan.part_rows)
                matrix = jnp.concatenate([message[rows, pl.ds(part * p, p)] for part in range(plan.rhs // p)], axis=0)
            children = [sent[k][level - 1][r:], rim[k][-1]] if k == 0 else [rim[k][-1], sent[k][level - 1][:r]]
            rim[k].append(dot(matrix, jnp.concatenate(children, axis=0)).astype(BF))

    def rim_gain(level, box):
        first, m = plan.first[level], plan.count[level]
        low = [sent[0][level][:r], sent[0][level][r:], rim[0][level]]
        high = [rim[1][level], sent[1][level][:r], sent[1][level][r:]]
        gain = None
        if box < 3:
            used = low[box : box + 2]
            gain = dot(masked[first + box, :, pl.ds(0, len(used) * r)], jnp.concatenate(used, axis=0))
        if box >= m - 3:
            from_end = box - (m - 3)
            used = high[max(from_end - 1, 0) : from_end + 1]
            start = (4 - len(used)) * r if from_end == 0 else 2 * r
            value = dot(masked[first + box, :, pl.ds(start, len(used) * r)], jnp.concatenate(used, axis=0))
            gain = value if gain is None else gain + value
        return gain

    for k in range(2):
        outermost[pl.ds(k * r, r)] = rim[k][FULL]
    for level in range(FULL):
        for box in plan.rim[level]:
            rows = pl.ds((plan.first[level] + box) * r, r)
            rims[pl.ds(plan.rim[level][box] * r, r)] = local[rows] + rim_gain(level, box)
    box = plan.first[LEVELS - 1]
    summit[...] = dot(masked[box, :, pl.ds(0, r)], below3[...]) + dot(masked[box, :, pl.ds(3 * r, r)], above3[...])


def final_kernel(
    plan, near, local, masked, edge_near, bs_t, ts_t, below2, above2, below, above, rims, outermost, partial,
    out, loc, stage, sems,
):
    p, r, n = plan.panels, plan.rank, plan.leaves
    rim_low, rim_high = outermost[pl.ds(0, r)], outermost[pl.ds(r, r)]

    def place(level, box):
        return pl.ds((plan.first[level] + box) * r, r)

    stack = jnp.concatenate([below2[pl.ds(r, r)], above2[pl.ds(r, r)]], axis=0)
    summit = (partial[...] + dot(masked[plan.first[LEVELS - 1], :, pl.ds(r, 2 * r)], stack)).astype(BF)
    pushed = dot(ts_t[plan.trans[LEVELS - 1]], summit)
    low, high = below[pl.ds(plan.msg_top, r)], above[pl.ds(plan.msg_top, r)]
    stacks = ([below2[pl.ds(0, r)], low, rim_high, high], [low, rim_low, high, above2[pl.ds(0, r)]])
    for k, stack in enumerate(stacks):
        gained = dot(masked[plan.first[FULL] + k], jnp.concatenate(stack, axis=0))
        loc[place(FULL, k)] = (gained + pushed[k * r : (k + 1) * r]).astype(BF)

    def descend(level, box):
        push = dot(ts_t[plan.trans[level] + box], loc[place(level, box)])
        for k in range(2):
            child = 2 * box + k
            edge = plan.rim[level - 1].get(child)
            own = local[place(level - 1, child)] if edge is None else rims[pl.ds(edge * r, r)]
            loc[place(level - 1, child)] = (own + push[k * r : (k + 1) * r]).astype(BF)

    for level in range(FULL, 1, -1):
        for box in range(plan.count[level]):
            descend(level, box)

    writes = []
    groups = sems.shape[0]
    per = n // groups

    def descend_group(group):
        for box in range(group * per // 2, (group + 1) * per // 2):
            descend(1, box)

    descend_group(0)
    for group in range(groups):
        if group + 1 < groups:
            descend_group(group + 1)
        for leaf in range(group * per, (group + 1) * per):
            total = near[pl.ds(leaf * p, p)].astype(F32) + dot(bs_t[leaf], loc[place(0, leaf)])
            if leaf == 0:
                total = total + dot(edge_near[0], below[pl.ds(0, p)])
            if leaf == n - 1:
                total = total + dot(edge_near[1], above[pl.ds(0, p)])
            stage[pl.ds(leaf * p, p)] = total.astype(BF)
        rows = pl.ds(group * per * p, per * p)
        copy = pltpu.make_async_copy(stage.at[rows], out.at[rows], sems.at[group])
        copy.start()
        writes.append(copy)
    for copy in writes:
        copy.wait()


def shifted(array, by):
    peers = lax.axis_size("slab")
    pairs = [(i, i + by) for i in range(peers) if 0 <= i + by < peers]
    return lax.ppermute(array, "slab", pairs)


def body(charges, near_blocks, near_pattern, leaf_basis, transfers, couplings, interactions):
    leaves, panels, rank, rhs = near_blocks.shape[0], near_blocks.shape[2], leaf_basis.shape[1], charges.shape[1]
    plan = Plan(leaves, panels, rank, rhs)
    hbm = pl.BlockSpec(memory_space=pltpu.HBM)
    vmem = pl.BlockSpec(memory_space=pltpu.VMEM)
    smem = pl.BlockSpec(memory_space=pltpu.SMEM)
    chunks = 8

    padded_x, poles, up, down, pair4, bs, ts = pl.pallas_call(
        lambda *refs: upward_kernel(plan, chunks, *refs),
        in_specs=[hbm, hbm, hbm],
        out_specs=[vmem] * 7,
        out_shape=[
            resident(((leaves + 2) * panels, rhs), BF),
            resident((plan.padded_boxes * rank, rhs), BF),
            resident((plan.msg_rows, rhs), BF),
            resident((plan.msg_rows, rhs), BF),
            resident((2 * rank, rhs), BF),
            resident(leaf_basis.shape, BF),
            resident(transfers.shape, BF),
        ],
        scratch_shapes=[pltpu.SemaphoreType.DMA((chunks + 2,))],
        compiler_params=pltpu.CompilerParams(vmem_limit_bytes=6 * MIB),
        name="upward",
    )(stay(charges), stay(leaf_basis), stay(transfers))

    below, above = shifted(up, 1), shifted(down, -1)

    local, masked, bs_t, ts_t, up2, down2, top = pl.pallas_call(
        lambda *refs: couple_kernel(plan, *refs),
        in_specs=[smem, vmem, vmem, vmem, vmem, vmem],
        out_specs=[vmem] * 7,
        out_shape=[
            resident((plan.inner_boxes * rank, rhs), F32),
            resident(couplings.shape, BF),
            resident((leaves, panels, rank), BF),
            resident((transfers.shape[0], panels, rank), BF),
            resident((2 * rank, rhs), BF),
            resident((2 * rank, rhs), BF),
            resident((rank, rhs), BF),
        ],
        compiler_params=pltpu.CompilerParams(vmem_limit_bytes=8 * MIB),
        cost_estimate=pl.CostEstimate(flops=6_000_000_000, bytes_accessed=8 * MIB, transcendentals=0),
        name="couple",
    )(interactions.T, keep(poles), keep(bs), keep(ts), keep(pair4), keep(couplings))

    below2, above2 = shifted(up2, 2), shifted(down2, -2)
    below3, above3 = shifted(top, 3), shifted(top, -3)

    near, edge_near = pl.pallas_call(
        lambda *refs: near_kernel(plan, *refs),
        in_specs=[smem, vmem, vmem],
        out_specs=[vmem] * 2,
        out_shape=[
            resident((leaves * panels, rhs), BF),
            resident((2, panels, panels), BF),
        ],
        compiler_params=pltpu.CompilerParams(vmem_limit_bytes=8 * MIB),
        cost_estimate=pl.CostEstimate(flops=6_000_000_000, bytes_accessed=8 * MIB, transcendentals=0),
        name="near",
    )(near_pattern.T, keep(padded_x), keep(near_blocks))

    rims, outermost, partial = pl.pallas_call(
        lambda *refs: rim_kernel(plan, *refs),
        in_specs=[vmem] * 6,
        out_specs=[vmem] * 3,
        out_shape=[
            resident((plan.rim_boxes * rank, rhs), F32),
            resident((2 * rank, rhs), BF),
            resident((rank, rhs), F32),
        ],
        compiler_params=pltpu.CompilerParams(vmem_limit_bytes=8 * MIB),
        cost_estimate=pl.CostEstimate(flops=10_000_000, bytes_accessed=MIB // 32, transcendentals=0),
        name="rim",
    )(keep(local), keep(masked), keep(below), keep(above), keep(below3), keep(above3))

    return pl.pallas_call(
        lambda *refs: final_kernel(plan, *refs),
        in_specs=[vmem] * 13,
        out_specs=hbm,
        out_shape=jax.ShapeDtypeStruct((leaves * panels, rhs), BF),
        scratch_shapes=[
            pltpu.VMEM((couplings.shape[0] * rank, rhs), BF),
            pltpu.VMEM((leaves * panels, rhs), BF),
            pltpu.SemaphoreType.DMA((leaves // 4,)),
        ],
        compiler_params=pltpu.CompilerParams(vmem_limit_bytes=14 * MIB),
        name="final",
    )(
        keep(near), keep(local), keep(masked), keep(edge_near), keep(bs_t), keep(ts_t),
        keep(below2), keep(above2), keep(below), keep(above), keep(rims), keep(outermost), keep(partial),
    )


def solution(mesh):
    spec = ("groups", "slab")
    in_specs = (
        P(spec, None),
        P(spec, None, None, None),
        P(spec, None),
        P(spec, None, None),
        P(spec, None, None),
        P(spec, None, None),
        P(spec, None),
    )
    return jax.shard_map(body, mesh=mesh, in_specs=in_specs, out_specs=P(spec, None), check_vma=False)
```

```python
import jax
import jax.numpy as jnp
from jax import lax
from jax.experimental import pallas as pl
from jax.experimental.pallas import tpu as pltpu
from jax.sharding import PartitionSpec as P

LEVELS = 6
FULL = LEVELS - 2
BF = jnp.bfloat16
F32 = jnp.float32
MIB = 1 << 20


def resident(shape, dtype):
    return pltpu.VMEM(shape, dtype)


def keep(array):
    return pltpu.with_memory_space_constraint(array, pltpu.VMEM)


def stay(array):
    return pltpu.with_memory_space_constraint(array, pltpu.HBM)


def dot(a, b):
    return lax.dot_general(a, b, (((1,), (0,)), ((), ())), preferred_element_type=F32)


class Plan:
    def __init__(self, leaves, panels, rank, rhs):
        self.leaves, self.panels, self.rank, self.rhs = leaves, panels, rank, rhs
        self.count = [leaves >> level for level in range(LEVELS)]
        self.first = [sum(self.count[:level]) for level in range(LEVELS)]
        self.trans = [0] + [sum(self.count[1:level]) for level in range(1, LEVELS)]
        self.padded = [sum(c + 6 for c in self.count[:level]) for level in range(FULL)]
        self.padded_boxes = sum(c + 6 for c in self.count[:FULL])
        self.inner_boxes = sum(self.count[:FULL])
        self.rim, self.rim_boxes = [], 0
        for m in self.count[:FULL]:
            boxes = sorted({0, 1, 2, m - 3, m - 2, m - 1})
            self.rim.append({box: self.rim_boxes + k for k, box in enumerate(boxes)})
            self.rim_boxes += len(boxes)
        self.msg_pole = [panels + 2 * rank * level for level in range(FULL)]
        self.msg_top = panels + 2 * rank * FULL
        self.msg_small = self.msg_top + rank
        self.msg_last = self.msg_small + rank
        self.part_rows = rank * panels // rhs
        self.msg_rows = self.msg_last + self.part_rows


def upward_kernel(plan, chunks, charges, basis, transfers, padded_x, poles, up, down, pair4, bs, ts, sems):
    p, r = plan.panels, plan.rank
    per = plan.leaves // chunks
    copies = []
    for c in range(chunks):
        rows = per * p
        copies.append(
            pltpu.make_async_copy(
                charges.at[pl.ds(c * rows, rows)], padded_x.at[pl.ds(p + c * rows, rows)], sems.at[c]
            )
        )
    basis_copy = pltpu.make_async_copy(basis, bs, sems.at[chunks])
    trans_copy = pltpu.make_async_copy(transfers, ts, sems.at[chunks + 1])
    basis_copy.start()
    copies[0].start()
    trans_copy.start()
    for copy in copies[1:]:
        copy.start()
    padded_x[pl.ds(0, p)] = jnp.zeros((p, plan.rhs), BF)
    padded_x[pl.ds(p * (plan.leaves + 1), p)] = jnp.zeros((p, plan.rhs), BF)
    for level in range(FULL):
        start = plan.padded[level] * r
        poles[pl.ds(start, 3 * r)] = jnp.zeros((3 * r, plan.rhs), BF)
        poles[pl.ds(start + (plan.count[level] + 3) * r, 3 * r)] = jnp.zeros((3 * r, plan.rhs), BF)
    basis_copy.wait()

    def keep(level, box, value):
        n = plan.count[level]
        if level < FULL:
            poles[pl.ds((plan.padded[level] + 3 + box) * r, r)] = value
            if n - 3 <= box <= n - 2:
                up[pl.ds(plan.msg_pole[level] + (box - n + 3) * r, r)] = value
            if 1 <= box <= 2:
                down[pl.ds(plan.msg_pole[level] + (box - 1) * r, r)] = value
        elif level == FULL:
            (up if box == 0 else down)[pl.ds(plan.msg_top, r)] = value
            pair4[pl.ds(box * r, r)] = value

    def climb(level, box):
        pair = poles[pl.ds((plan.padded[level - 1] + 3 + 2 * box) * r, 2 * r)]
        keep(level, box, dot(ts[plan.trans[level] + box], pair).astype(BF))

    done = [0] * (FULL + 1)

    def climb_ready():
        ready = list(done)
        for level in range(1, FULL + 1):
            while 2 * done[level] + 2 <= ready[level - 1]:
                climb(level, done[level])
                done[level] += 1

    for c in range(chunks):
        copies[c].wait()
        if c == 1:
            trans_copy.wait()
        climb_ready()
        for leaf in range(c * per, (c + 1) * per):
            x = padded_x[pl.ds(p * (leaf + 1), p)]
            keep(0, leaf, dot(bs[leaf], x).astype(BF))
        done[0] = (c + 1) * per
    while done[FULL] < plan.count[FULL]:
        climb_ready()
    for message, leaf, last in ((up, plan.leaves - 1, True), (down, 0, False)):
        message[pl.ds(0, p)] = padded_x[pl.ds(p * (leaf + 1), p)]
        message[pl.ds(plan.msg_small, r), pl.ds(0, p)] = bs[leaf]
        for level in range(1, FULL):
            box = plan.count[level] - 1 if last else 0
            message[pl.ds(plan.msg_small, r), pl.ds(level * p, p)] = ts[plan.trans[level] + box]
        matrix = plan.trans[FULL] + (plan.count[FULL] - 1 if last else 0)
        rows = plan.part_rows
        for part in range(plan.rhs // p):
            message[pl.ds(plan.msg_last, rows), pl.ds(part * p, p)] = ts[matrix, pl.ds(part * rows, rows)]


def couple_kernel(
    plan, flags, poles, bs, ts, pair4, couplings,
    local, masked, bs_t, ts_t, up2, down2, top,
):
    p, r = plan.panels, plan.rank
    summit = dot(ts[plan.trans[LEVELS - 1]], pair4[...]).astype(BF)
    up2[pl.ds(0, r)] = pair4[pl.ds(r, r)]
    down2[pl.ds(0, r)] = pair4[pl.ds(0, r)]
    for message in (up2, down2):
        message[pl.ds(r, r)] = summit
    top[...] = summit
    for box in range(ts.shape[0]):
        ts_t[box] = ts[box].T
    for leaf in range(bs.shape[0]):
        bs_t[leaf] = bs[leaf].T
    lane = lax.broadcasted_iota(jnp.int32, (r, 4 * r), 1)

    def mask(box):
        low = jnp.where(lane < r, flags[0, box], flags[1, box])
        high = jnp.where(lane < 3 * r, flags[2, box], flags[3, box])
        chosen = jnp.where(lane < 2 * r, low, high)
        value = couplings[box] * chosen.astype(F32).astype(BF)
        masked[box] = value
        return value

    for level in range(FULL):
        for box in range(plan.count[level]):
            row = (plan.padded[level] + box) * r
            stack = jnp.concatenate([poles[pl.ds(row, 2 * r)], poles[pl.ds(row + 5 * r, 2 * r)]], axis=0)
            index = plan.first[level] + box
            local[pl.ds(index * r, r)] = dot(mask(index), stack)
    for box in range(plan.inner_boxes, sum(plan.count)):
        mask(box)


def near_kernel(plan, pattern, padded_x, near_blocks, near, edge_near):
    p = plan.panels

    def side(leaf, slot):
        block = near_blocks[leaf, slot]
        return jnp.where(pattern[slot, leaf] != 0, block, jnp.zeros_like(block))

    zero = jnp.zeros((p, p), BF)
    for leaf in range(0, plan.leaves, 2):
        upper = jnp.concatenate([side(leaf, 0), near_blocks[leaf, 1], side(leaf, 2), zero], axis=1)
        lower = jnp.concatenate([zero, side(leaf + 1, 0), near_blocks[leaf + 1, 1], side(leaf + 1, 2)], axis=1)
        both = jnp.concatenate([upper, lower], axis=0)
        near[pl.ds(leaf * p, 2 * p)] = dot(both, padded_x[pl.ds(leaf * p, 4 * p)]).astype(BF)
    edge_near[0] = side(0, 0)
    edge_near[1] = side(plan.leaves - 1, 2)


def rim_kernel(plan, local, masked, below, above, below3, above3, rims, outermost, summit):
    p, r = plan.panels, plan.rank
    small = pl.ds(plan.msg_small, r)
    messages = (below, above)

    sent = [[message[pl.ds(plan.msg_pole[level], 2 * r)] for level in range(FULL)] for message in messages]
    rim = [[dot(message[small, pl.ds(0, p)], message[pl.ds(0, p)]).astype(BF)] for message in messages]
    for level in range(1, FULL + 1):
        for k, message in enumerate(messages):
            if level < FULL:
                matrix = message[small, pl.ds(level * p, p)]
            else:
                rows = pl.ds(plan.msg_last, plan.part_rows)
                matrix = jnp.concatenate([message[rows, pl.ds(part * p, p)] for part in range(plan.rhs // p)], axis=0)
            children = [sent[k][level - 1][r:], rim[k][-1]] if k == 0 else [rim[k][-1], sent[k][level - 1][:r]]
            rim[k].append(dot(matrix, jnp.concatenate(children, axis=0)).astype(BF))

    def rim_gain(level, box):
        first, m = plan.first[level], plan.count[level]
        low = [sent[0][level][:r], sent[0][level][r:], rim[0][level]]
        high = [rim[1][level], sent[1][level][:r], sent[1][level][r:]]
        gain = None
        if box < 3:
            used = low[box : box + 2]
            gain = dot(masked[first + box, :, pl.ds(0, len(used) * r)], jnp.concatenate(used, axis=0))
        if box >= m - 3:
            from_end = box - (m - 3)
            used = high[max(from_end - 1, 0) : from_end + 1]
            start = (4 - len(used)) * r if from_end == 0 else 2 * r
            value = dot(masked[first + box, :, pl.ds(start, len(used) * r)], jnp.concatenate(used, axis=0))
            gain = value if gain is None else gain + value
        return gain

    for k in range(2):
        outermost[pl.ds(k * r, r)] = rim[k][FULL]
    for level in range(FULL):
        for box in plan.rim[level]:
            rows = pl.ds((plan.first[level] + box) * r, r)
            rims[pl.ds(plan.rim[level][box] * r, r)] = local[rows] + rim_gain(level, box)
    box = plan.first[LEVELS - 1]
    summit[...] = dot(masked[box, :, pl.ds(0, r)], below3[...]) + dot(masked[box, :, pl.ds(3 * r, r)], above3[...])


def final_kernel(
    plan, near, local, masked, edge_near, bs_t, ts_t, below2, above2, below, above, rims, outermost, partial,
    out, loc, stage, sems,
):
    p, r, n = plan.panels, plan.rank, plan.leaves
    rim_low, rim_high = outermost[pl.ds(0, r)], outermost[pl.ds(r, r)]

    def place(level, box):
        return pl.ds((plan.first[level] + box) * r, r)

    stack = jnp.concatenate([below2[pl.ds(r, r)], above2[pl.ds(r, r)]], axis=0)
    summit = (partial[...] + dot(masked[plan.first[LEVELS - 1], :, pl.ds(r, 2 * r)], stack)).astype(BF)
    pushed = dot(ts_t[plan.trans[LEVELS - 1]], summit)
    low, high = below[pl.ds(plan.msg_top, r)], above[pl.ds(plan.msg_top, r)]
    stacks = ([below2[pl.ds(0, r)], low, rim_high, high], [low, rim_low, high, above2[pl.ds(0, r)]])
    for k, stack in enumerate(stacks):
        gained = dot(masked[plan.first[FULL] + k], jnp.concatenate(stack, axis=0))
        loc[place(FULL, k)] = (gained + pushed[k * r : (k + 1) * r]).astype(BF)

    def descend(level, box):
        push = dot(ts_t[plan.trans[level] + box], loc[place(level, box)])
        for k in range(2):
            child = 2 * box + k
            edge = plan.rim[level - 1].get(child)
            own = local[place(level - 1, child)] if edge is None else rims[pl.ds(edge * r, r)]
            loc[place(level - 1, child)] = (own + push[k * r : (k + 1) * r]).astype(BF)

    for level in range(FULL, 1, -1):
        for box in range(plan.count[level]):
            descend(level, box)

    writes = []
    groups = sems.shape[0]
    per = n // groups

    def descend_group(group):
        for box in range(group * per // 2, (group + 1) * per // 2):
            descend(1, box)

    descend_group(0)
    for group in range(groups):
        if group + 1 < groups:
            descend_group(group + 1)
        for leaf in range(group * per, (group + 1) * per):
            total = near[pl.ds(leaf * p, p)].astype(F32) + dot(bs_t[leaf], loc[place(0, leaf)])
            if leaf == 0:
                total = total + dot(edge_near[0], below[pl.ds(0, p)])
            if leaf == n - 1:
                total = total + dot(edge_near[1], above[pl.ds(0, p)])
            stage[pl.ds(leaf * p, p)] = total.astype(BF)
        rows = pl.ds(group * per * p, per * p)
        copy = pltpu.make_async_copy(stage.at[rows], out.at[rows], sems.at[group])
        copy.start()
        writes.append(copy)
    for copy in writes:
        copy.wait()


def shifted(array, by):
    peers = lax.axis_size("slab")
    pairs = [(i, i + by) for i in range(peers) if 0 <= i + by < peers]
    return lax.ppermute(array, "slab", pairs)


def body(charges, near_blocks, near_pattern, leaf_basis, transfers, couplings, interactions):
    leaves, panels, rank, rhs = near_blocks.shape[0], near_blocks.shape[2], leaf_basis.shape[1], charges.shape[1]
    plan = Plan(leaves, panels, rank, rhs)
    hbm = pl.BlockSpec(memory_space=pltpu.HBM)
    vmem = pl.BlockSpec(memory_space=pltpu.VMEM)
    smem = pl.BlockSpec(memory_space=pltpu.SMEM)
    chunks = 16

    padded_x, poles, up, down, pair4, bs, ts = pl.pallas_call(
        lambda *refs: upward_kernel(plan, chunks, *refs),
        in_specs=[hbm, hbm, hbm],
        out_specs=[vmem] * 7,
        out_shape=[
            resident(((leaves + 2) * panels, rhs), BF),
            resident((plan.padded_boxes * rank, rhs), BF),
            resident((plan.msg_rows, rhs), BF),
            resident((plan.msg_rows, rhs), BF),
            resident((2 * rank, rhs), BF),
            resident(leaf_basis.shape, BF),
            resident(transfers.shape, BF),
        ],
        scratch_shapes=[pltpu.SemaphoreType.DMA((chunks + 2,))],
        compiler_params=pltpu.CompilerParams(vmem_limit_bytes=6 * MIB),
        name="upward",
    )(stay(charges), stay(leaf_basis), stay(transfers))

    below, above = shifted(up, 1), shifted(down, -1)

    local, masked, bs_t, ts_t, up2, down2, top = pl.pallas_call(
        lambda *refs: couple_kernel(plan, *refs),
        in_specs=[smem, vmem, vmem, vmem, vmem, vmem],
        out_specs=[vmem] * 7,
        out_shape=[
            resident((plan.inner_boxes * rank, rhs), F32),
            resident(couplings.shape, BF),
            resident((leaves, panels, rank), BF),
            resident((transfers.shape[0], panels, rank), BF),
            resident((2 * rank, rhs), BF),
            resident((2 * rank, rhs), BF),
            resident((rank, rhs), BF),
        ],
        compiler_params=pltpu.CompilerParams(vmem_limit_bytes=8 * MIB),
        cost_estimate=pl.CostEstimate(flops=6_000_000_000, bytes_accessed=8 * MIB, transcendentals=0),
        name="couple",
    )(interactions.T, keep(poles), keep(bs), keep(ts), keep(pair4), keep(couplings))

    below2, above2 = shifted(up2, 2), shifted(down2, -2)
    below3, above3 = shifted(top, 3), shifted(top, -3)

    near, edge_near = pl.pallas_call(
        lambda *refs: near_kernel(plan, *refs),
        in_specs=[smem, vmem, vmem],
        out_specs=[vmem] * 2,
        out_shape=[
            resident((leaves * panels, rhs), BF),
            resident((2, panels, panels), BF),
        ],
        compiler_params=pltpu.CompilerParams(vmem_limit_bytes=8 * MIB),
        cost_estimate=pl.CostEstimate(flops=6_000_000_000, bytes_accessed=8 * MIB, transcendentals=0),
        name="near",
    )(near_pattern.T, keep(padded_x), keep(near_blocks))

    rims, outermost, partial = pl.pallas_call(
        lambda *refs: rim_kernel(plan, *refs),
        in_specs=[vmem] * 6,
        out_specs=[vmem] * 3,
        out_shape=[
            resident((plan.rim_boxes * rank, rhs), F32),
            resident((2 * rank, rhs), BF),
            resident((rank, rhs), F32),
        ],
        compiler_params=pltpu.CompilerParams(vmem_limit_bytes=8 * MIB),
        cost_estimate=pl.CostEstimate(flops=10_000_000, bytes_accessed=MIB // 32, transcendentals=0),
        name="rim",
    )(keep(local), keep(masked), keep(below), keep(above), keep(below3), keep(above3))

    return pl.pallas_call(
        lambda *refs: final_kernel(plan, *refs),
        in_specs=[vmem] * 13,
        out_specs=hbm,
        out_shape=jax.ShapeDtypeStruct((leaves * panels, rhs), BF),
        scratch_shapes=[
            pltpu.VMEM((couplings.shape[0] * rank, rhs), BF),
            pltpu.VMEM((leaves * panels, rhs), BF),
            pltpu.SemaphoreType.DMA((leaves // 4,)),
        ],
        compiler_params=pltpu.CompilerParams(vmem_limit_bytes=14 * MIB),
        name="final",
    )(
        keep(near), keep(local), keep(masked), keep(edge_near), keep(bs_t), keep(ts_t),
        keep(below2), keep(above2), keep(below), keep(above), keep(rims), keep(outermost), keep(partial),
    )


def solution(mesh):
    spec = ("groups", "slab")
    in_specs = (
        P(spec, None),
        P(spec, None, None, None),
        P(spec, None),
        P(spec, None, None),
        P(spec, None, None),
        P(spec, None, None),
        P(spec, None),
    )
    return jax.shard_map(body, mesh=mesh, in_specs=in_specs, out_specs=P(spec, None), check_vma=False)
```

```python
import jax
import jax.numpy as jnp
from jax import lax
from jax.experimental import pallas as pl
from jax.experimental.pallas import tpu as pltpu
from jax.sharding import PartitionSpec as P

LEVELS = 6
FULL = LEVELS - 2
BF = jnp.bfloat16
F32 = jnp.float32
MIB = 1 << 20


def resident(shape, dtype):
    return pltpu.VMEM(shape, dtype)


def keep(array):
    return pltpu.with_memory_space_constraint(array, pltpu.VMEM)


def stay(array):
    return pltpu.with_memory_space_constraint(array, pltpu.HBM)


def dot(a, b):
    return lax.dot_general(a, b, (((1,), (0,)), ((), ())), preferred_element_type=F32)


class Plan:
    def __init__(self, leaves, panels, rank, rhs):
        self.leaves, self.panels, self.rank, self.rhs = leaves, panels, rank, rhs
        self.count = [leaves >> level for level in range(LEVELS)]
        self.first = [sum(self.count[:level]) for level in range(LEVELS)]
        self.trans = [0] + [sum(self.count[1:level]) for level in range(1, LEVELS)]
        self.padded = [sum(c + 6 for c in self.count[:level]) for level in range(FULL)]
        self.padded_boxes = sum(c + 6 for c in self.count[:FULL])
        self.inner_boxes = sum(self.count[:FULL])
        self.rim, self.rim_boxes = [], 0
        for m in self.count[:FULL]:
            boxes = sorted({0, 1, 2, m - 3, m - 2, m - 1})
            self.rim.append({box: self.rim_boxes + k for k, box in enumerate(boxes)})
            self.rim_boxes += len(boxes)
        self.msg_pole = [panels + 2 * rank * level for level in range(FULL)]
        self.msg_top = panels + 2 * rank * FULL
        self.msg_small = self.msg_top + rank
        self.msg_last = self.msg_small + rank
        self.part_rows = rank * panels // rhs
        self.msg_rows = self.msg_last + self.part_rows


def upward_kernel(plan, chunks, charges, basis, transfers, padded_x, poles, up, down, pair4, bs, ts, sems):
    p, r = plan.panels, plan.rank
    per = plan.leaves // chunks
    copies = []
    for c in range(chunks):
        rows = per * p
        copies.append(
            pltpu.make_async_copy(
                charges.at[pl.ds(c * rows, rows)], padded_x.at[pl.ds(p + c * rows, rows)], sems.at[c]
            )
        )
    basis_copy = pltpu.make_async_copy(basis, bs, sems.at[chunks])
    trans_copy = pltpu.make_async_copy(transfers, ts, sems.at[chunks + 1])
    basis_copy.start()
    copies[0].start()
    trans_copy.start()
    for copy in copies[1:]:
        copy.start()
    padded_x[pl.ds(0, p)] = jnp.zeros((p, plan.rhs), BF)
    padded_x[pl.ds(p * (plan.leaves + 1), p)] = jnp.zeros((p, plan.rhs), BF)
    for level in range(FULL):
        start = plan.padded[level] * r
        poles[pl.ds(start, 3 * r)] = jnp.zeros((3 * r, plan.rhs), BF)
        poles[pl.ds(start + (plan.count[level] + 3) * r, 3 * r)] = jnp.zeros((3 * r, plan.rhs), BF)
    basis_copy.wait()

    def keep(level, box, value):
        n = plan.count[level]
        if level < FULL:
            poles[pl.ds((plan.padded[level] + 3 + box) * r, r)] = value
            if n - 3 <= box <= n - 2:
                up[pl.ds(plan.msg_pole[level] + (box - n + 3) * r, r)] = value
            if 1 <= box <= 2:
                down[pl.ds(plan.msg_pole[level] + (box - 1) * r, r)] = value
        elif level == FULL:
            (up if box == 0 else down)[pl.ds(plan.msg_top, r)] = value
            pair4[pl.ds(box * r, r)] = value

    def climb(level, box):
        pair = poles[pl.ds((plan.padded[level - 1] + 3 + 2 * box) * r, 2 * r)]
        keep(level, box, dot(ts[plan.trans[level] + box], pair).astype(BF))

    done = [0] * (FULL + 1)

    def climb_ready():
        ready = list(done)
        for level in range(1, FULL + 1):
            while 2 * done[level] + 2 <= ready[level - 1]:
                climb(level, done[level])
                done[level] += 1

    for c in range(chunks):
        copies[c].wait()
        if c == 1:
            trans_copy.wait()
        climb_ready()
        for leaf in range(c * per, (c + 1) * per):
            x = padded_x[pl.ds(p * (leaf + 1), p)]
            keep(0, leaf, dot(bs[leaf], x).astype(BF))
        done[0] = (c + 1) * per
    while done[FULL] < plan.count[FULL]:
        climb_ready()
    for message, leaf, last in ((up, plan.leaves - 1, True), (down, 0, False)):
        message[pl.ds(0, p)] = padded_x[pl.ds(p * (leaf + 1), p)]
        message[pl.ds(plan.msg_small, r), pl.ds(0, p)] = bs[leaf]
        for level in range(1, FULL):
            box = plan.count[level] - 1 if last else 0
            message[pl.ds(plan.msg_small, r), pl.ds(level * p, p)] = ts[plan.trans[level] + box]
        matrix = plan.trans[FULL] + (plan.count[FULL] - 1 if last else 0)
        rows = plan.part_rows
        for part in range(plan.rhs // p):
            message[pl.ds(plan.msg_last, rows), pl.ds(part * p, p)] = ts[matrix, pl.ds(part * rows, rows)]


def couple_kernel(
    plan, flags, poles, bs, ts, pair4, couplings,
    local, masked, bs_t, ts_t, up2, down2, top,
):
    p, r = plan.panels, plan.rank
    summit = dot(ts[plan.trans[LEVELS - 1]], pair4[...]).astype(BF)
    up2[pl.ds(0, r)] = pair4[pl.ds(r, r)]
    down2[pl.ds(0, r)] = pair4[pl.ds(0, r)]
    for message in (up2, down2):
        message[pl.ds(r, r)] = summit
    top[...] = summit
    for box in range(ts.shape[0]):
        ts_t[box] = ts[box].T
    for leaf in range(bs.shape[0]):
        bs_t[leaf] = bs[leaf].T
    lane = lax.broadcasted_iota(jnp.int32, (r, 4 * r), 1)

    def mask(box):
        low = jnp.where(lane < r, flags[0, box], flags[1, box])
        high = jnp.where(lane < 3 * r, flags[2, box], flags[3, box])
        chosen = jnp.where(lane < 2 * r, low, high)
        value = couplings[box] * chosen.astype(F32).astype(BF)
        masked[box] = value
        return value

    for level in range(FULL):
        for box in range(plan.count[level]):
            row = (plan.padded[level] + box) * r
            stack = jnp.concatenate([poles[pl.ds(row, 2 * r)], poles[pl.ds(row + 5 * r, 2 * r)]], axis=0)
            index = plan.first[level] + box
            local[pl.ds(index * r, r)] = dot(mask(index), stack)
    for box in range(plan.inner_boxes, sum(plan.count)):
        mask(box)


def near_kernel(plan, pattern, padded_x, near_blocks, near, edge_near):
    p = plan.panels

    def side(leaf, slot):
        block = near_blocks[leaf, slot]
        return jnp.where(pattern[slot, leaf] != 0, block, jnp.zeros_like(block))

    zero = jnp.zeros((p, p), BF)
    for leaf in range(0, plan.leaves, 2):
        upper = jnp.concatenate([side(leaf, 0), near_blocks[leaf, 1], side(leaf, 2), zero], axis=1)
        lower = jnp.concatenate([zero, side(leaf + 1, 0), near_blocks[leaf + 1, 1], side(leaf + 1, 2)], axis=1)
        both = jnp.concatenate([upper, lower], axis=0)
        near[pl.ds(leaf * p, 2 * p)] = dot(both, padded_x[pl.ds(leaf * p, 4 * p)]).astype(BF)
    edge_near[0] = side(0, 0)
    edge_near[1] = side(plan.leaves - 1, 2)


def rim_kernel(plan, local, masked, below, above, below3, above3, rims, outermost, summit):
    p, r = plan.panels, plan.rank
    small = pl.ds(plan.msg_small, r)
    messages = (below, above)

    sent = [[message[pl.ds(plan.msg_pole[level], 2 * r)] for level in range(FULL)] for message in messages]
    rim = [[dot(message[small, pl.ds(0, p)], message[pl.ds(0, p)]).astype(BF)] for message in messages]
    for level in range(1, FULL + 1):
        for k, message in enumerate(messages):
            if level < FULL:
                matrix = message[small, pl.ds(level * p, p)]
            else:
                rows = pl.ds(plan.msg_last, plan.part_rows)
                matrix = jnp.concatenate([message[rows, pl.ds(part * p, p)] for part in range(plan.rhs // p)], axis=0)
            children = [sent[k][level - 1][r:], rim[k][-1]] if k == 0 else [rim[k][-1], sent[k][level - 1][:r]]
            rim[k].append(dot(matrix, jnp.concatenate(children, axis=0)).astype(BF))

    def rim_gain(level, box):
        first, m = plan.first[level], plan.count[level]
        low = [sent[0][level][:r], sent[0][level][r:], rim[0][level]]
        high = [rim[1][level], sent[1][level][:r], sent[1][level][r:]]
        gain = None
        if box < 3:
            used = low[box : box + 2]
            gain = dot(masked[first + box, :, pl.ds(0, len(used) * r)], jnp.concatenate(used, axis=0))
        if box >= m - 3:
            from_end = box - (m - 3)
            used = high[max(from_end - 1, 0) : from_end + 1]
            start = (4 - len(used)) * r if from_end == 0 else 2 * r
            value = dot(masked[first + box, :, pl.ds(start, len(used) * r)], jnp.concatenate(used, axis=0))
            gain = value if gain is None else gain + value
        return gain

    for k in range(2):
        outermost[pl.ds(k * r, r)] = rim[k][FULL]
    for level in range(FULL):
        for box in plan.rim[level]:
            rows = pl.ds((plan.first[level] + box) * r, r)
            rims[pl.ds(plan.rim[level][box] * r, r)] = local[rows] + rim_gain(level, box)
    box = plan.first[LEVELS - 1]
    summit[...] = dot(masked[box, :, pl.ds(0, r)], below3[...]) + dot(masked[box, :, pl.ds(3 * r, r)], above3[...])


def final_kernel(
    plan, near, local, masked, edge_near, bs_t, ts_t, below2, above2, below, above, rims, outermost, partial,
    out, loc, stage, sems,
):
    p, r, n = plan.panels, plan.rank, plan.leaves
    rim_low, rim_high = outermost[pl.ds(0, r)], outermost[pl.ds(r, r)]

    def place(level, box):
        return pl.ds((plan.first[level] + box) * r, r)

    stack = jnp.concatenate([below2[pl.ds(r, r)], above2[pl.ds(r, r)]], axis=0)
    summit = (partial[...] + dot(masked[plan.first[LEVELS - 1], :, pl.ds(r, 2 * r)], stack)).astype(BF)
    pushed = dot(ts_t[plan.trans[LEVELS - 1]], summit)
    low, high = below[pl.ds(plan.msg_top, r)], above[pl.ds(plan.msg_top, r)]
    stacks = ([below2[pl.ds(0, r)], low, rim_high, high], [low, rim_low, high, above2[pl.ds(0, r)]])
    for k, stack in enumerate(stacks):
        gained = dot(masked[plan.first[FULL] + k], jnp.concatenate(stack, axis=0))
        loc[place(FULL, k)] = (gained + pushed[k * r : (k + 1) * r]).astype(BF)

    def descend(level, box):
        push = dot(ts_t[plan.trans[level] + box], loc[place(level, box)])
        for k in range(2):
            child = 2 * box + k
            edge = plan.rim[level - 1].get(child)
            own = local[place(level - 1, child)] if edge is None else rims[pl.ds(edge * r, r)]
            loc[place(level - 1, child)] = (own + push[k * r : (k + 1) * r]).astype(BF)

    for level in range(FULL, 1, -1):
        for box in range(plan.count[level]):
            descend(level, box)

    writes = []
    groups = sems.shape[0]
    per = n // groups

    def descend_group(group):
        for box in range(group * per // 2, (group + 1) * per // 2):
            descend(1, box)

    descend_group(0)
    for group in range(groups):
        if group + 1 < groups:
            descend_group(group + 1)
        for leaf in range(group * per, (group + 1) * per):
            total = near[pl.ds(leaf * p, p)].astype(F32) + dot(bs_t[leaf], loc[place(0, leaf)])
            if leaf == 0:
                total = total + dot(edge_near[0], below[pl.ds(0, p)])
            if leaf == n - 1:
                total = total + dot(edge_near[1], above[pl.ds(0, p)])
            stage[pl.ds(leaf * p, p)] = total.astype(BF)
        rows = pl.ds(group * per * p, per * p)
        copy = pltpu.make_async_copy(stage.at[rows], out.at[rows], sems.at[group])
        copy.start()
        writes.append(copy)
    for copy in writes:
        copy.wait()


def shifted(array, by):
    peers = lax.axis_size("slab")
    pairs = [(i, i + by) for i in range(peers) if 0 <= i + by < peers]
    return lax.ppermute(array, "slab", pairs)


def body(charges, near_blocks, near_pattern, leaf_basis, transfers, couplings, interactions):
    leaves, panels, rank, rhs = near_blocks.shape[0], near_blocks.shape[2], leaf_basis.shape[1], charges.shape[1]
    plan = Plan(leaves, panels, rank, rhs)
    hbm = pl.BlockSpec(memory_space=pltpu.HBM)
    vmem = pl.BlockSpec(memory_space=pltpu.VMEM)
    smem = pl.BlockSpec(memory_space=pltpu.SMEM)
    chunks = 4

    padded_x, poles, up, down, pair4, bs, ts = pl.pallas_call(
        lambda *refs: upward_kernel(plan, chunks, *refs),
        in_specs=[hbm, hbm, hbm],
        out_specs=[vmem] * 7,
        out_shape=[
            resident(((leaves + 2) * panels, rhs), BF),
            resident((plan.padded_boxes * rank, rhs), BF),
            resident((plan.msg_rows, rhs), BF),
            resident((plan.msg_rows, rhs), BF),
            resident((2 * rank, rhs), BF),
            resident(leaf_basis.shape, BF),
            resident(transfers.shape, BF),
        ],
        scratch_shapes=[pltpu.SemaphoreType.DMA((chunks + 2,))],
        compiler_params=pltpu.CompilerParams(vmem_limit_bytes=6 * MIB),
        name="upward",
    )(stay(charges), stay(leaf_basis), stay(transfers))

    below, above = shifted(up, 1), shifted(down, -1)

    local, masked, bs_t, ts_t, up2, down2, top = pl.pallas_call(
        lambda *refs: couple_kernel(plan, *refs),
        in_specs=[smem, vmem, vmem, vmem, vmem, vmem],
        out_specs=[vmem] * 7,
        out_shape=[
            resident((plan.inner_boxes * rank, rhs), F32),
            resident(couplings.shape, BF),
            resident((leaves, panels, rank), BF),
            resident((transfers.shape[0], panels, rank), BF),
            resident((2 * rank, rhs), BF),
            resident((2 * rank, rhs), BF),
            resident((rank, rhs), BF),
        ],
        compiler_params=pltpu.CompilerParams(vmem_limit_bytes=8 * MIB),
        cost_estimate=pl.CostEstimate(flops=6_000_000_000, bytes_accessed=8 * MIB, transcendentals=0),
        name="couple",
    )(interactions.T, keep(poles), keep(bs), keep(ts), keep(pair4), keep(couplings))

    below2, above2 = shifted(up2, 2), shifted(down2, -2)
    below3, above3 = shifted(top, 3), shifted(top, -3)

    near, edge_near = pl.pallas_call(
        lambda *refs: near_kernel(plan, *refs),
        in_specs=[smem, vmem, vmem],
        out_specs=[vmem] * 2,
        out_shape=[
            resident((leaves * panels, rhs), BF),
            resident((2, panels, panels), BF),
        ],
        compiler_params=pltpu.CompilerParams(vmem_limit_bytes=8 * MIB),
        cost_estimate=pl.CostEstimate(flops=6_000_000_000, bytes_accessed=8 * MIB, transcendentals=0),
        name="near",
    )(near_pattern.T, keep(padded_x), keep(near_blocks))

    rims, outermost, partial = pl.pallas_call(
        lambda *refs: rim_kernel(plan, *refs),
        in_specs=[vmem] * 6,
        out_specs=[vmem] * 3,
        out_shape=[
            resident((plan.rim_boxes * rank, rhs), F32),
            resident((2 * rank, rhs), BF),
            resident((rank, rhs), F32),
        ],
        compiler_params=pltpu.CompilerParams(vmem_limit_bytes=8 * MIB),
        cost_estimate=pl.CostEstimate(flops=10_000_000, bytes_accessed=MIB // 32, transcendentals=0),
        name="rim",
    )(keep(local), keep(masked), keep(below), keep(above), keep(below3), keep(above3))

    return pl.pallas_call(
        lambda *refs: final_kernel(plan, *refs),
        in_specs=[vmem] * 13,
        out_specs=hbm,
        out_shape=jax.ShapeDtypeStruct((leaves * panels, rhs), BF),
        scratch_shapes=[
            pltpu.VMEM((couplings.shape[0] * rank, rhs), BF),
            pltpu.VMEM((leaves * panels, rhs), BF),
            pltpu.SemaphoreType.DMA((leaves // 4,)),
        ],
        compiler_params=pltpu.CompilerParams(vmem_limit_bytes=14 * MIB),
        name="final",
    )(
        keep(near), keep(local), keep(masked), keep(edge_near), keep(bs_t), keep(ts_t),
        keep(below2), keep(above2), keep(below), keep(above), keep(rims), keep(outermost), keep(partial),
    )


def solution(mesh):
    spec = ("groups", "slab")
    in_specs = (
        P(spec, None),
        P(spec, None, None, None),
        P(spec, None),
        P(spec, None, None),
        P(spec, None, None),
        P(spec, None, None),
        P(spec, None),
    )
    return jax.shard_map(body, mesh=mesh, in_specs=in_specs, out_specs=P(spec, None), check_vma=False)
```
